128 devices in a mesh: tm: 8 (over z_lo, y), space: 16 (over x, z_hi, core).
Axes of the slice: x: 4, y: 4, z: 4 (z_hi: 2, z_lo: 2; z = z_hi * 2 + z_lo), core: 2. Of those that a mesh axis runs over, the one named last changes fastest.
Arguments:
- start: float32 [16, 3, 8, 64, 1024], P(None, None, 'tm', 'space'), may hold values from -400 to 400
- smear_links: float32 [3, 3, 3, 8, 64, 1024], P(None, None, None, 'tm', 'space'), may hold values from -1 to 1, as said below
- fat_links: float32 [4, 3, 3, 8, 64, 1024], P(None, None, None, 'tm', 'space'), may hold values from -1 to 1, as said below
- naik_links: float32 [4, 3, 3, 8, 64, 1024], P(None, None, None, 'tm', 'space'), may hold values from -1 to 1, as said below
Outputs:
- projected: float32 [8, 16, 16], P('tm')
- solution: float32 [16, 3, 64, 64, 128], P(None, None, 'space', 'tm')
The draws below stay inside these ranges and needn't reach their ends.
Inputs may be any that keep to these rules, and one draw needn't show every extreme that they name: `smear_links`: every link is a real orthogonal 3 x 3 matrix of determinant one. `fat_links`: every link is a real orthogonal 3 x 3 matrix of determinant one. `naik_links`: every link is a real orthogonal 3 x 3 matrix of determinant one.
All inputs are finite; a program needn't handle non-finite values.
Results may differ from the reference program's by a relative error of at most 0.0003.
Values sent between devices are 32-bit elements; how exact they have to be, the bound alone decides.
A program may use at most 128 MiB of HBM per device.

```python
import math
import jax
import jax.numpy as jnp
from jax import lax

NV = 16
Z = 16
CHEB = 3
ITERS = 2
T_SIZE = 8
L = 64


def rotations(key, lead):
    keys = jax.random.split(key, 3)
    first = jax.random.uniform(keys[0], lead, jnp.float32, -math.pi, math.pi)
    second = jax.random.uniform(keys[1], lead, jnp.float32, -math.pi, math.pi)
    third = jax.random.uniform(keys[2], lead, jnp.float32, -math.pi, math.pi)
    ca, sa = (jnp.cos(first), jnp.sin(first))
    cb, sb = (jnp.cos(second), jnp.sin(second))
    cg, sg = (jnp.cos(third), jnp.sin(third))
    rows = [[ca * cb * cg - sa * sg, -ca * cb * sg - sa * cg, ca * sb], [sa * cb * cg + ca * sg, -sa * cb * sg + ca * cg, sa * sb], [-sb * cg, sb * sg, cb]]
    return jnp.stack([jnp.stack(entries, axis=1) for entries in rows], axis=1)


def draw_smear_links(key, part):
    key = jax.random.fold_in(key, 11)
    return rotations(key, (3, T_SIZE, L, L * Z))


def draw_fat_links(key, part):
    key = jax.random.fold_in(key, 12)
    return rotations(key, (4, T_SIZE, L, L * Z))


def draw_naik_links(key, part):
    key = jax.random.fold_in(key, 13)
    return rotations(key, (4, T_SIZE, L, L * Z))


def draw_start(key, part):
    key = jax.random.fold_in(key, 14)
    keys = jax.random.split(key, 3)
    site_scale = jnp.exp(jax.random.uniform(keys[0], (1, 1, T_SIZE, L, L, 1), jnp.float32, 0.0, math.log(10.0)))
    column_scale = jnp.exp(jax.random.uniform(keys[1], (NV, 1, 1, 1, 1, 1), jnp.float32, 0.0, math.log(10.0)))
    values = jnp.clip(jax.random.normal(keys[2], (NV, 3, T_SIZE, L, L, Z), jnp.float32), -4.0, 4.0)
    return (values * site_scale * column_scale).reshape(NV, 3, T_SIZE, L, L * Z)


def setup_inputs(seed: int = 0) -> dict:
    key_list = jax.random.split(jax.random.key(seed), 5)
    start = draw_start(jax.random.fold_in(key_list[4], 71), 0)
    smear_links = draw_smear_links(jax.random.fold_in(key_list[4], 71), 0)
    fat_links = draw_fat_links(jax.random.fold_in(key_list[4], 71), 0)
    naik_links = draw_naik_links(jax.random.fold_in(key_list[4], 71), 0)
    return dict(start=start, smear_links=smear_links, fat_links=fat_links, naik_links=naik_links)


HIGH = lax.Precision.HIGHEST
CENTER = 6.5
HALF_WIDTH = 5.5
MASS = 0.5
ONE_HOP = 1.125
THREE_HOP = -1.0 / 24.0

def turn(links, field):
    return jnp.stack([links[a, 0] * field[:, 0] + links[a, 1] * field[:, 1] + links[a, 2] * field[:, 2] for a in range(3)], axis=1)

def turn_back(links, field):
    return jnp.stack([links[0, a] * field[:, 0] + links[1, a] * field[:, 1] + links[2, a] * field[:, 2] for a in range(3)], axis=1)

def shift_z(field, step, zlen):
    length = field.shape[-1]
    zpos = jnp.arange(length) % zlen
    ahead = jnp.roll(field, -step, axis=-1)
    if step > 0:
        return jnp.where(zpos + step < zlen, ahead, jnp.roll(field, zlen - step, axis=-1))
    return jnp.where(zpos + step >= 0, ahead, jnp.roll(field, -step - zlen, axis=-1))

def shift_time(field, step, zlen):
    width = abs(step) * zlen
    zeros = jnp.zeros(field.shape[:-1] + (width,), field.dtype)
    if step > 0:
        return jnp.concatenate([field[..., width:], zeros], axis=-1)
    return jnp.concatenate([zeros, field[..., :-width]], axis=-1)

def alternate(values, shape):
    return jnp.broadcast_to(1 - 2 * (values % 2), shape).astype(jnp.float32)

def geometry(tpos, xpos, ypos, zpos, shape):
    signs = [jnp.ones(shape, jnp.float32), alternate(xpos, shape), alternate(xpos + ypos, shape), alternate(xpos + ypos + zpos, shape)]
    even = jnp.broadcast_to((tpos + xpos + ypos + zpos) % 2 == 0, shape).astype(jnp.float32)
    return (signs, even)

def lower_inverse(gram):
    lower = jnp.linalg.cholesky(gram)
    ident = jnp.broadcast_to(jnp.eye(gram.shape[-1], dtype=jnp.float32), gram.shape)
    return lax.linalg.triangular_solve(lower, ident, left_side=True, lower=True)

def laplace(field, links):
    total = 6.0 * field
    total = total - (turn(links[0], jnp.roll(field, -1, axis=2)) + jnp.roll(turn_back(links[0], field), 1, axis=2))
    total = total - (turn(links[1], jnp.roll(field, -Z, axis=3)) + jnp.roll(turn_back(links[1], field), Z, axis=3))
    total = total - (turn(links[2], shift_z(field, 1, Z)) + shift_z(turn_back(links[2], field), -1, Z))
    return total

def filter_slice(pair):
    start, links = pair
    count = 3.0 * L * L * Z

    def sigma(field):
        return (laplace(field, links) - CENTER * field) / HALF_WIDTH
    earlier = start
    current = sigma(start)
    for step in range(CHEB - 1):
        earlier, current = (current, 2.0 * sigma(current) - earlier)
    gram = jnp.einsum('kcxs,jcxs->kj', current, current, precision=HIGH) / count
    inverse = lower_inverse(gram)
    basis = jnp.einsum('kj,jcxs->kcxs', inverse, current, precision=HIGH)
    image = laplace(basis, links)
    projected = jnp.einsum('kcxs,jcxs->kj', basis, image, precision=HIGH) / count
    return (basis, projected)

def hop(field, fat, naik, signs):
    total = jnp.zeros_like(field)
    for mu in range(4):
        for links, depth, weight in ((fat, 1, ONE_HOP), (naik, 3, THREE_HOP)):
            back = turn_back(links[mu], field)
            if mu == 0:
                ahead = jnp.roll(field, -depth, axis=2)
                behind = jnp.roll(back, depth, axis=2)
            elif mu == 1:
                ahead = jnp.roll(field, -depth, axis=3)
                behind = jnp.roll(back, depth, axis=3)
            elif mu == 2:
                ahead = shift_z(field, depth, Z)
                behind = shift_z(back, -depth, Z)
            else:
                ahead = shift_time(field, depth, Z)
                behind = shift_time(back, -depth, Z)
            total = total + weight * signs[mu] * (turn(links[mu], ahead) - behind)
    return 0.5 * total

def block_order(links):
    return links.reshape(4, 3, 3, T_SIZE, L, L, Z).transpose(0, 1, 2, 4, 5, 3, 6).reshape(4, 3, 3, L, L, T_SIZE * Z)

def reference(start, smear_links, fat_links, naik_links):
    basis, projected = lax.map(filter_slice, (jnp.moveaxis(start, 2, 0), jnp.moveaxis(smear_links, 3, 0)))
    basis = basis.reshape(T_SIZE, NV, 3, L, L, Z).transpose(1, 2, 3, 4, 0, 5).reshape(NV, 3, L, L, T_SIZE * Z)
    fat = block_order(fat_links)
    naik = block_order(naik_links)
    xpos = jnp.arange(L)[:, None, None]
    ypos = jnp.arange(L)[None, :, None]
    cells = jnp.arange(T_SIZE * Z)[None, None, :]
    signs, even = geometry(cells // Z, xpos, ypos, cells % Z, (L, L, T_SIZE * Z))

    def normal(field):
        return MASS * MASS * field - hop(hop(field, fat, naik, signs), fat, naik, signs)

    def solve(source):
        rhs = source[None] * even
        solution = jnp.zeros_like(rhs)
        resid = rhs
        direc = rhs
        norm_now = jnp.sum(resid * resid)
        for step in range(ITERS):
            image = normal(direc)
            alpha = norm_now / jnp.sum(direc * image)
            solution = solution + alpha * direc
            if step + 1 < ITERS:
                resid = resid - alpha * image
                norm_next = jnp.sum(resid * resid)
                direc = resid + norm_next / norm_now * direc
                norm_now = norm_next
        return solution[0]
    solution = lax.map(solve, basis)
    return (projected, solution)
```

```python
import functools
import jax
import jax.numpy as jnp
from jax import lax
from jax.sharding import PartitionSpec as P
import jax.experimental.pallas as pl
import jax.experimental.pallas.tpu as pltpu

MESH = pl.DeviceIdType.MESH
HIGH = lax.Precision.HIGHEST
F32 = jnp.float32
CENTER = 6.5
HALF_WIDTH = 5.5
ONE_HOP = 1.125
THREE_HOP = -1.0 / 24.0
SITES = 196608.0

ZP, ZM, PK, SKL, SUB, DSK, DSKS, CC, CT1, CT3, CZ1, CZ3, ZZ, EX, SLOTS = (
    0, 1, 2, 4, 5, 6, 7, 8, 10, 12, 14, 16, 18, 26, 28)


def lanes(v, idx):
    return jnp.take_along_axis(v, idx, axis=1, mode="promise_in_bounds")


def rows(v, idx):
    return jnp.take_along_axis(v, idx, axis=0, mode="promise_in_bounds")


def tile_iota():
    row = lax.broadcasted_iota(jnp.int32, (8, 128), 0)
    lane = lax.broadcasted_iota(jnp.int32, (8, 128), 1)
    return row, lane


def mul_add(acc, links, field, back):
    out = []
    for a in range(3):
        total = acc[a]
        for b in range(3):
            total = total + links[b * 3 + a if back else a * 3 + b] * field[b]
        out.append(total)
    return out


def fill_positions(ix, t):
    row, lane = tile_iota()
    chunk = lane >> 4
    low = lane & 15
    zc = lane & 7
    ix[ZP] = (chunk << 4) | ((low + 1) & 15)
    ix[ZM] = (chunk << 4) | ((low - 1) & 15)
    ysrc = (chunk - t) & 7
    for par in range(2):
        ix[PK + par] = (ysrc << 4) | (zc << 1) | ((t + par + ysrc) & 1)
    ix[SKL] = (((chunk - row) & 7) << 4) | low
    ix[SUB] = (chunk - row) & 7
    ix[DSK] = (((chunk + row) & 7) << 4) | low
    ix[DSKS] = (((chunk + row) & 7) << 4) | (low ^ 8)
    for rho in range(2):
        z = (zc << 1) | ((chunk + row + rho) & 1)
        ix[CC + rho] = (((chunk + row) & 7) << 4) | z
        ix[CT1 + rho] = (((chunk + row - 1) & 7) << 4) | z
        ix[CT3 + rho] = (((chunk + row - 3) & 7) << 4) | z
        ix[CZ1 + rho] = (((chunk + row) & 7) << 4) | ((z - 1) & 15)
        ix[CZ3 + rho] = (((chunk + row) & 7) << 4) | ((z - 3) & 15)
        for j, d in enumerate((1, -1, 3, -3)):
            ix[ZZ + rho * 4 + j] = (lane & 120) | (((z + d) & 15) >> 1)
    ix[EX] = (chunk << 4) | (low >> 1)
    ix[EX + 1] = (chunk << 4) | 8 | (low >> 1)


def kernel(start_ref, smear_ref, fat_ref, naik_ref, proj_ref, out_ref,
           raw, sraw, yy, sx, syz, hh, af, prod, fs, fr, lraw, lxh, lyh, tl, tx, tyh, ll,
           ee, hn, hp, h2, fp, fps, ix, cb, mom, gone, gslot, gtm, kone, kslot, sone, sslot, stm,
           in_sem, y_send, y_recv, sx_send, sx_recv, l_send, l_recv, l_own, lh_send, lh_recv,
           f_send, f_recv, f_own, dx_send, dx_recv, dy_send, dy_recv,
           c_send, c_recv, r_send, r_recv, t_send, t_recv):
    t = lax.axis_index("tm")
    s = lax.axis_index("space")
    core = s & 1
    chip = s >> 1
    nxt = (t, (s + 1) & 15)
    prv = (t, (s + 15) & 15)
    ynxt = ((t + 1) & 7, s)
    yprv = ((t + 7) & 7, s)
    partner = (t, s + 1 - 2 * core)
    chips = [(t, (s + 2 * j) & 15) for j in range(1, 8)]
    times = [((t + d) & 7, s) for d in range(1, 8)]

    def remote(src, dst, send, recv, dev):
        return pltpu.make_async_remote_copy(src, dst, send, recv, device_id=dev, device_id_type=MESH)

    load_start = pltpu.make_async_copy(start_ref, raw, in_sem.at[0])
    load_smear = pltpu.make_async_copy(smear_ref, sraw, in_sem.at[1])
    load_start.start()
    load_smear.start()
    own_links = [
        pltpu.make_async_copy(ref.at[:, t], lraw.at[t, pl.ds(36 * i, 36)], l_own.at[i])
        for i, ref in enumerate((fat_ref, naik_ref))
    ]
    for c in own_links:
        c.start()

    barrier = pltpu.get_barrier_semaphore()
    friends = [nxt, prv] + chips + times
    for dev in friends:
        pl.semaphore_signal(barrier, inc=1, device_id=dev, device_id_type=MESH)

    fill_positions(ix, t)
    row, lane = tile_iota()
    high_half = (lane & 8) != 0

    load_start.wait()

    def place_start(i, _):
        for x in range(4):
            yy[0, 1 + x, i] = raw[pl.ds(i * 32 + x, 8, stride=4), :]
        return 0

    lax.fori_loop(0, 48, place_start, 0, unroll=4)
    pl.semaphore_wait(barrier, len(friends))

    def halo(n):
        return [
            remote(yy.at[n, 4], yy.at[n, 0], y_send.at[n, 0], y_recv.at[n, 0], nxt),
            remote(yy.at[n, 1], yy.at[n, 5], y_send.at[n, 1], y_recv.at[n, 1], prv),
        ]

    halos = halo(0)
    for c in halos:
        c.start()

    load_smear.wait()

    def ahead_y(v):
        r = pltpu.roll(v, 112, 1)
        return jnp.where(lane < 112, r, pltpu.roll(r, 7, 0))

    def behind_y(v):
        r = pltpu.roll(v, 16, 1)
        return jnp.where(lane >= 16, r, pltpu.roll(r, 1, 0))

    zp_i = ix[ZP]
    zm_i = ix[ZM]

    def place_smear(i, _):
        for x in range(4):
            sx[1 + x, i] = sraw[pl.ds(i * 32 + x, 8, stride=4), :]
            ly = sraw[pl.ds((9 + i) * 32 + x, 8, stride=4), :]
            lz = sraw[pl.ds((18 + i) * 32 + x, 8, stride=4), :]
            syz[x, 0, i] = ly
            syz[x, 1, i] = behind_y(ly)
            syz[x, 2, i] = lz
            syz[x, 3, i] = lanes(lz, zm_i)
        return 0

    lax.fori_loop(0, 9, place_smear, 0)
    sx_copy = remote(sx.at[4], sx.at[0], sx_send, sx_recv, nxt)
    sx_copy.start()

    link_copies = []
    for d in range(1, 8):
        dest = (t + d) & 7
        for i, ref in enumerate((fat_ref, naik_ref)):
            c = remote(ref.at[:, dest], lraw.at[t, pl.ds(36 * i, 36)],
                       l_send.at[i, d - 1], l_recv.at[i, d - 1], (dest, s))
            c.start()
            link_copies.append(c)

    def local_pass(n):
        def step(i, _):
            x = i >> 2
            base = (i & 3) * 12
            field = [[yy[n, 1 + x, base + v * 3 + c] for c in range(3)] for v in range(4)]
            acc = [[jnp.zeros((8, 128), F32)] * 3 for _ in range(4)]
            for d in range(4):
                links = [syz[x, d, e] for e in range(9)]
                for v in range(4):
                    if d == 0:
                        moved = [ahead_y(f) for f in field[v]]
                    elif d == 1:
                        moved = [behind_y(f) for f in field[v]]
                    else:
                        moved = [lanes(f, zp_i if d == 2 else zm_i) for f in field[v]]
                    acc[v] = mul_add(acc[v], links, moved, d & 1)
            for v in range(4):
                for c in range(3):
                    hh[x, base + v * 3 + c] = acc[v][c]
            return 0

        lax.fori_loop(0, 16, step, 0)

    def x_pass(n, plane_of, count, finish):
        def step(i, _):
            x = plane_of(i >> 2)
            base = (i & 3) * 12
            for back in (False, True):
                links = [sx[x if back else 1 + x, e] for e in range(9)]
                for v in range(4):
                    field = [yy[n, x if back else 2 + x, base + v * 3 + c] for c in range(3)]
                    acc = [hh[x, base + v * 3 + c] for c in range(3)] if not back else keep[v]
                    acc = mul_add(acc, links, field, back)
                    if not back:
                        if v == 0:
                            keep = []
                        keep.append(acc)
                    else:
                        for c in range(3):
                            finish(x, base + v * 3 + c, acc[c])
            return 0

        lax.fori_loop(0, 4 * count, step, 0)

    for n in range(3):
        local_pass(n)
        if n == 0:
            sx_copy.wait()
        for c in halos:
            c.wait()

        def finish(x, comp, acc, n=n):
            if n == 0:
                value = (-0.5 / HALF_WIDTH) * yy[0, 1 + x, comp] - (1.0 / HALF_WIDTH) * acc
            else:
                value = ((-1.0 / HALF_WIDTH) * yy[n, 1 + x, comp] - (2.0 / HALF_WIDTH) * acc
                         - yy[n - 1, 1 + x, comp])
            yy[n + 1, 1 + x, comp] = value

        x_pass(n, lambda i: 3 * i, 2, finish)
        if n < 2:
            halos = halo(n + 1)
            for c in halos:
                c.start()
        x_pass(n, lambda i: 1 + i, 2, finish)
        if n == 1:
            for c in own_links + link_copies:
                c.wait()
            link_halos = []
            for i in range(2):
                link_halos.append(remote(lraw.at[:, pl.ds(36 * i, 9)], lxh.at[:, pl.ds(9 * i, 9)],
                                         lh_send.at[0, i], lh_recv.at[0, i], nxt))
                link_halos.append(remote(lraw.at[:, pl.ds(36 * i + 9, 9)], lyh.at[:, pl.ds(9 * i, 9)],
                                         lh_send.at[1, i], lh_recv.at[1, i], ynxt))
            for c in link_halos:
                c.start()

    def pack(i, _):
        x = i >> 3
        pair = i & 7
        idx = ix[PK + (x & 1)]
        for c in range(3):
            one = lanes(yy[3, 1 + x, pair * 3 + c], idx)
            two = lanes(yy[3, 1 + x, pair * 3 + 24 + c], idx)
            fs[pl.ds(x * 24 + pair * 3 + c, 8, stride=96), :] = jnp.where(high_half, two, one)
        return 0

    lax.fori_loop(0, 32, pack, 0)

    def part(ref, which):
        return ref.at[pl.ds(pl.multiple_of(which * 96, 96), 96)]

    f_copies = [
        remote(part(fs, (t + d) & 7), part(fr, t), f_send.at[d - 1], f_recv.at[d - 1], times[d - 1])
        for d in range(1, 8)
    ]
    for c in f_copies:
        c.start()
    f_local = pltpu.make_async_copy(part(fs, t), part(fr, t), f_own)
    f_local.start()

    def products(left, right):
        def step(k, _):
            mine = [left(x, k * 3 + c) for x in range(4) for c in range(3)]
            for d in range(9):
                j = (k + d) & 15
                total = None
                for x in range(4):
                    for c in range(3):
                        term = mine[x * 3 + c] * right(x, j * 3 + c)
                        total = term if total is None else total + term
                total = jnp.sum(total, axis=0, keepdims=True)
                prod[pl.ds(j * 16 + k, 1), :] = total
                prod[pl.ds(k * 16 + j, 1), :] = total
            return 0

        lax.fori_loop(0, 16, step, 0)
        sums = lax.dot_general(jnp.ones((8, 128), F32), prod[...], (((1,), (1,)), ((), ())),
                               precision=HIGH, preferred_element_type=F32)
        return jnp.where(row == 0, sums[:, :128], sums[:, 128:])

    def to_partner(buf, which):
        return remote(buf.at[0], buf.at[1], c_send.at[which], c_recv.at[which], partner)

    def to_chips(buf, which):
        return [remote(buf.at[chip], buf.at[chip], r_send.at[which, j], r_recv.at[which, j], chips[j])
                for j in range(7)]

    def to_times(buf, which):
        return [remote(buf.at[t], buf.at[t], t_send.at[which, j], t_recv.at[which, j], times[j])
                for j in range(7)]

    def total_of(buf):
        total = buf[0]
        for j in range(1, 8):
            total = total + buf[j]
        return total

    gone[0] = products(lambda x, e: yy[3, 1 + x, e], lambda x, e: yy[3, 1 + x, e])
    g_partner = to_partner(gone, 0)
    g_partner.start()
    halos = halo(3)
    for c in halos:
        c.start()

    def turned(ref, first, stride):
        v = lanes(ref[pl.ds(first, 8, stride=stride), :], ix[SKL])
        return rows(v, ix[SUB])

    lflat = lraw.reshape(8 * 72 * 4, 128)
    xflat = lxh.reshape(8 * 18 * 4, 128)
    yflat = lyh.reshape(8 * 18 * 4, 128)

    def place_links(i, _):
        for x in range(4):
            tl[x, i] = turned(lflat, i * 4 + x, 288)
        return 0

    lax.fori_loop(0, 72, place_links, 0)
    g_partner.wait()
    gslot[chip] = gone[0] + gone[1]
    g_chips = to_chips(gslot, 0)
    for c in g_chips:
        c.start()

    for c in link_halos:
        c.wait()

    def place_link_halos(i, _):
        for x in range(4):
            tx[x, i] = turned(xflat, i * 4 + x, 72)
            tyh[x, i] = turned(yflat, i * 4 + x, 72)
        return 0

    lax.fori_loop(0, 18, place_link_halos, 0)
    for c in g_chips:
        c.wait()
    gtm[t] = total_of(gslot)
    g_times = to_times(gtm, 0)
    for c in g_times:
        c.start()

    chunk = lane >> 4

    def fill_links(i, _):
        x = i & 3
        e = i >> 2
        xsign = (1 - 2 * (x & 1)).astype(F32)
        ysign = (1 - 2 * (row & 1)).astype(F32)
        tsign = (1 - 2 * (chunk & 1)).astype(F32)
        for kind, hop, weight in ((0, 1, 0.5 * ONE_HOP), (1, 3, 0.5 * THREE_HOP)):
            off = 36 * kind
            px = x - hop
            own = [tl[x, off + 9 * mu + e] for mu in range(4)]
            before_x = jnp.where(px >= 0, tl[jnp.maximum(px, 0), off + e],
                                 tx[jnp.minimum(px + 4, 3), 9 * kind + e])
            before_y = pltpu.roll(jnp.where(row < 8 - hop, own[1], tyh[x, 9 * kind + e]), hop, 0)
            for pi in range(2):
                rho = (x + pi) & 1
                cc = ix[CC + rho]
                ct = ix[(CT3 if kind else CT1) + rho]
                cz = ix[(CZ3 if kind else CZ1) + rho]
                pis = -1.0 if pi else 1.0
                scale = [
                    jnp.full((8, 128), weight, F32),
                    jnp.full((8, 128), weight, F32) * xsign,
                    weight * xsign * ysign,
                ]
                fwd = [lanes(own[mu], cc) for mu in range(4)]
                bwd = [lanes(before_x, cc), lanes(before_y, ct), lanes(own[2], cz), lanes(own[3], ct)]
                for mu in range(4):
                    if mu < 3:
                        up, down = scale[mu], -scale[mu]
                    else:
                        up = jnp.where(chunk < 8 - hop, (pis * weight) * tsign, 0.0)
                        down = jnp.where(chunk >= hop, (-pis * weight) * tsign, 0.0)
                    ll[pi, x, (mu * 2 + kind) * 2, e] = up * fwd[mu]
                    ll[pi, x, (mu * 2 + kind) * 2 + 1, e] = down * bwd[mu]
        return 0

    lax.fori_loop(0, 36, fill_links, 0)

    for c in f_copies:
        c.wait()
    f_local.wait()

    def unpack(i, _):
        x = i >> 3
        for c in range(3):
            e = (i & 7) * 3 + c
            v = rows(fr[pl.ds(x * 24 + e, 8, stride=96), :], ix[SUB])
            fp[x, e] = lanes(v, ix[DSK])
            fps[x, e] = lanes(v, ix[DSKS])
        return 0

    lax.fori_loop(0, 32, unpack, 0)

    for c in g_times:
        c.wait()

    flat = gtm.reshape(64, 128)
    expand = jnp.where(chunk == row, 1.0 / SITES, 0.0).astype(F32)
    for half in range(2):
        cb[pl.ds(128 * half, 128), :] = lax.dot_general(
            flat[pl.ds(half, 8, stride=8), :], jnp.where(chunk == row, 1.0, 0.0).astype(F32),
            (((0,), (0,)), ((), ())), precision=HIGH, preferred_element_type=F32)
    cols = [cb[pl.ds(16 * m, 16), :] * (1.0 / SITES) for m in range(16)]
    line = lax.broadcasted_iota(jnp.int32, (16, 128), 0)
    inv = [jnp.where(line == m, 1.0, 0.0).astype(F32) for m in range(16)]
    for j in range(16):
        scale = 1.0 / jnp.sqrt(cols[j][j:j + 1])
        factor = jnp.where(line > j, cols[j] * scale, 0.0)
        for m in range(j + 1, 16):
            cols[m] = cols[m] - factor * (cols[m][j:j + 1] * scale)
        for m in range(j + 1):
            top = inv[m][j:j + 1] * scale
            inv[m] = jnp.where(line == j, top, inv[m] - factor * top)
    for m in range(16):
        cb[pl.ds(16 * m, 16), :] = inv[m]

    def entry(k, j):
        return jnp.broadcast_to(cb[pl.ds(16 * j + k, 1), :], (8, 128))

    for pair in range(8):
        same = [jnp.where(high_half, entry(pair + 8, j + 8), entry(pair, j)) for j in range(pair + 1)]
        cross = [jnp.where(high_half, entry(pair + 8, j), 0.0) for j in range(8)]

        def mix(x, total, pair=pair, same=same, cross=cross):
            for c in range(3):
                value = cross[0] * fps[x, c]
                for j in range(1, 8):
                    value = value + cross[j] * fps[x, j * 3 + c]
                for j in range(pair + 1):
                    value = value + same[j] * fp[x, j * 3 + c]
                ee[0, 3 + x, pair * 3 + c] = value
                total = total + value * value
            return total

        mom[0, pair] = lax.fori_loop(0, 4, mix, jnp.zeros((8, 128), F32))

    def d_halo(n):
        return [
            remote(ee.at[n, pl.ds(4, 3)], ee.at[n, pl.ds(0, 3)], dx_send.at[n, 0], dx_recv.at[n, 0], nxt),
            remote(ee.at[n, pl.ds(3, 3)], ee.at[n, pl.ds(7, 3)], dx_send.at[n, 1], dx_recv.at[n, 1], prv),
            remote(ee.at[n, pl.ds(3, 4), :, pl.ds(5, 3)], hp.at[n, :, :, pl.ds(5, 3)],
                   dy_send.at[n, 0], dy_recv.at[n, 0], ynxt),
            remote(ee.at[n, pl.ds(3, 4), :, pl.ds(0, 3)], hn.at[n, :, :, pl.ds(0, 3)],
                   dy_send.at[n, 1], dy_recv.at[n, 1], yprv),
        ]

    def inner_pass(n, pi):
        def step(i, _):
            x = i >> 1
            base = (i & 1) * 12
            rho = (x + pi) & 1
            field = [[ee[n, 3 + x, base + v * 3 + c] for c in range(3)] for v in range(4)]
            acc = [[jnp.zeros((8, 128), F32)] * 3 for _ in range(4)]
            for d in range(8, 16):
                links = [ll[pi, x, d, e] for e in range(9)]
                hop = 3 if (d >> 1) & 1 else 1
                if d < 12:
                    idx = ix[ZZ + rho * 4 + (d - 8)]
                for v in range(4):
                    if d < 12:
                        moved = [lanes(f, idx) for f in field[v]]
                    else:
                        shift = 16 * hop if d & 1 else 128 - 16 * hop
                        moved = [pltpu.roll(f, shift, 1) for f in field[v]]
                    acc[v] = mul_add(acc[v], links, moved, d & 1)
            for v in range(4):
                for c in range(3):
                    h2[x, base + v * 3 + c] = acc[v][c]
            return 0

        lax.fori_loop(0, 8, step, 0)

    def outer_pass(n, pi, store):
        for pair in range(8):
            mom[n + 1, pair] = jnp.zeros((8, 128), F32)

        def step(i, _):
            x = i >> 1
            base = (i & 1) * 12
            acc = [[h2[x, base + v * 3 + c] for c in range(3)] for v in range(4)]
            for d in range(8):
                links = [ll[pi, x, d, e] for e in range(9)]
                hop = 3 if (d >> 1) & 1 else 1
                for v in range(4):
                    comps = [base + v * 3 + c for c in range(3)]
                    if d < 4:
                        moved = [ee[n, 3 + x - hop if d & 1 else 3 + x + hop, e] for e in comps]
                    elif d & 1:
                        moved = [pltpu.roll(jnp.where(row < 8 - hop, ee[n, 3 + x, e], hp[n, x, e]), hop, 0)
                                 for e in comps]
                    else:
                        moved = [pltpu.roll(jnp.where(row >= hop, ee[n, 3 + x, e], hn[n, x, e]), 8 - hop, 0)
                                 for e in comps]
                    acc[v] = mul_add(acc[v], links, moved, d & 1)
            for v in range(4):
                for c in range(3):
                    if store:
                        ee[n + 1, 3 + x, base + v * 3 + c] = acc[v][c]
                mom[n + 1, (i & 1) * 4 + v] += (
                    acc[v][0] * acc[v][0] + acc[v][1] * acc[v][1] + acc[v][2] * acc[v][2])
            return 0

        lax.fori_loop(0, 8, step, 0)

    def flat_to_square(tile):
        total = jnp.zeros((16, 128), F32)
        for m in range(16):
            piece = jnp.broadcast_to(tile[m >> 3:(m >> 3) + 1], (16, 128))
            piece = pltpu.roll(piece, (128 - 16 * (m & 7)) & 127, 1) if m & 7 else piece
            total = jnp.where(line == m, piece, total)
        return total[:, :16]

    for n in range(3):
        pi = 1 - (n & 1)
        d_copies = d_halo(n)
        for c in d_copies:
            c.start()
        inner_pass(n, pi)
        if n == 0:
            local_pass(3)
            for c in halos:
                c.wait()

            def keep_image(x, comp, acc):
                af[x, comp] = 6.0 * yy[3, 1 + x, comp] - acc

            x_pass(3, lambda i: i, 4, keep_image)
            kone[0] = products(lambda x, e: yy[3, 1 + x, e], lambda x, e: af[x, e])
            k_partner = to_partner(kone, 1)
            k_partner.start()
        if n == 1:
            k_partner.wait()
            kslot[chip] = kone[0] + kone[1]
            k_chips = to_chips(kslot, 1)
            for c in k_chips:
                c.start()
        if n == 2:
            for c in k_chips:
                c.wait()
            square = flat_to_square(total_of(kslot)) * (1.0 / SITES)
            pick = jnp.where(lane == t * 16, 1.0, 0.0).astype(F32)
            weights = lax.dot_general(pick, cb[...], (((1,), (1,)), ((), ())),
                                      precision=HIGH, preferred_element_type=F32)
            weights = flat_to_square(jnp.where(row == 0, weights[:, :128], weights[:, 128:]))
            half = lax.dot_general(weights, square, (((0,), (0,)), ((), ())),
                                   precision=HIGH, preferred_element_type=F32)
            proj_ref[0] = lax.dot_general(half, weights, (((1,), (0,)), ((), ())),
                                          precision=HIGH, preferred_element_type=F32)
        for c in d_copies:
            c.wait()
        outer_pass(n, pi, n < 2)

    prod[...] = jnp.zeros((256, 128), F32)
    for m in range(4):
        for pair in range(8):
            prod[pl.ds(8 * m + pair, 1), :] = jnp.sum(mom[m, pair], axis=0, keepdims=True)
    select = jnp.where(((lane >> 3) & 1) == row, 1.0, 0.0).astype(F32)
    sone[0] = lax.dot_general(select, prod[pl.ds(0, 128), :], (((1,), (1,)), ((), ())),
                              precision=HIGH, preferred_element_type=F32)
    s_partner = to_partner(sone, 2)
    s_partner.start()
    s_partner.wait()
    sslot[chip] = sone[0] + sone[1]
    s_chips = to_chips(sslot, 2)
    for c in s_chips:
        c.start()
    for c in s_chips:
        c.wait()
    stm[t] = total_of(sslot)
    s_times = to_times(stm, 1)
    for c in s_times:
        c.start()
    for c in s_times:
        c.wait()
    n0 = total_of(stm)
    n1 = pltpu.roll(n0, 120, 1)
    n2 = pltpu.roll(n0, 112, 1)
    n3 = pltpu.roll(n0, 104, 1)
    ratio = n1 / n0
    alpha0 = 1.0 / (0.25 + ratio)
    rr = alpha0 * alpha0 * (n2 - ratio * n1)
    beta = rr / n0
    a = alpha0 * ratio + beta
    energy = 0.25 * rr * (1.0 + beta) + a * a * n1 - 2.0 * a * alpha0 * n2 + alpha0 * alpha0 * n3
    alpha1 = rr / energy
    first = alpha0 + alpha1 * a
    second = alpha1 * alpha0

    def spread(v, pair):
        low = jnp.broadcast_to(v[0:1, pair:pair + 1], (8, 128))
        high = jnp.broadcast_to(v[1:2, pair:pair + 1], (8, 128))
        return jnp.where(high_half, high, low)

    for pair in range(8):
        ca = spread(first, pair)
        cd = spread(second, pair)

        def finish_out(x, _, pair=pair, ca=ca, cd=cd):
            even = ((x + row + chunk + lane) & 1) == 0
            for c in range(3):
                value = ca * ee[0, 3 + x, pair * 3 + c] + cd * ee[2, 3 + x, pair * 3 + c]
                out_ref[pair, c, x] = jnp.where(even, lanes(value, ix[EX]), 0.0)
                out_ref[pair + 8, c, x] = jnp.where(even, lanes(value, ix[EX + 1]), 0.0)
            return 0

        lax.fori_loop(0, 4, finish_out, 0)


def rows_first(array, lead):
    return array.reshape(lead, 4, 8, 128).transpose(0, 2, 1, 3)


def body(start, smear_links, fat_links, naik_links):
    start = rows_first(start, 48).reshape(1536, 128)
    smear = rows_first(smear_links, 27).reshape(864, 128)
    fat = rows_first(fat_links, 36)
    naik = rows_first(naik_links, 36)
    vm = lambda *shape: pltpu.VMEM(shape, F32)
    dma = lambda *shape: pltpu.SemaphoreType.DMA(shape) if shape else pltpu.SemaphoreType.DMA
    anywhere = pl.BlockSpec(memory_space=pl.ANY)
    local = pl.BlockSpec(memory_space=pltpu.VMEM)
    return pl.pallas_call(
        kernel,
        out_shape=(jax.ShapeDtypeStruct((1, 16, 16), F32),
                   jax.ShapeDtypeStruct((16, 3, 4, 8, 128), F32)),
        in_specs=[anywhere] * 4,
        out_specs=(local, local),
        scratch_shapes=[
            vm(1536, 128), vm(864, 128), vm(4, 6, 48, 8, 128), vm(5, 9, 8, 128), vm(4, 4, 9, 8, 128),
            vm(4, 48, 8, 128), vm(4, 48, 8, 128), vm(256, 128), vm(768, 128), vm(768, 128),
            vm(8, 72, 4, 128), vm(8, 18, 4, 128), vm(8, 18, 4, 128),
            vm(4, 72, 8, 128), vm(4, 18, 8, 128), vm(4, 18, 8, 128), vm(2, 4, 16, 9, 8, 128),
            vm(3, 10, 24, 8, 128), vm(3, 4, 24, 8, 128), vm(3, 4, 24, 8, 128), vm(4, 24, 8, 128),
            vm(4, 24, 8, 128), vm(4, 24, 8, 128), pltpu.VMEM((SLOTS, 8, 128), jnp.int32),
            vm(256, 128), vm(4, 8, 8, 128),
            vm(2, 8, 128), vm(8, 8, 128), vm(8, 8, 128),
            vm(2, 8, 128), vm(8, 8, 128),
            vm(2, 8, 128), vm(8, 8, 128), vm(8, 8, 128),
            dma(2), dma(4, 2), dma(4, 2), dma(), dma(), dma(2, 7), dma(2, 7), dma(2),
            dma(2, 2), dma(2, 2), dma(7), dma(7), dma(),
            dma(3, 2), dma(3, 2), dma(3, 2), dma(3, 2),
            dma(3), dma(3), dma(3, 7), dma(3, 7), dma(2, 7), dma(2, 7),
        ],
        compiler_params=pltpu.CompilerParams(
            collective_id=0, has_side_effects=True, vmem_limit_bytes=40 * 2**20),
        name="distill",
    )(start, smear, fat, naik)


def solution(mesh):
    in_specs = (
        P(None, None, "tm", "space", None),
        P(None, None, None, "tm", "space", None),
        P(None, None, None, "tm", "space", None),
        P(None, None, None, "tm", "space", None),
    )
    out_specs = (P("tm", None, None), P(None, None, "space", "tm", None))
    return jax.shard_map(body, mesh=mesh, in_specs=in_specs, out_specs=out_specs, check_vma=False)
```

```python
import functools
import jax
import jax.numpy as jnp
from jax import lax
from jax.sharding import PartitionSpec as P
import jax.experimental.pallas as pl
import jax.experimental.pallas.tpu as pltpu

MESH = pl.DeviceIdType.MESH
HIGH = lax.Precision.HIGHEST
F32 = jnp.float32
CENTER = 6.5
HALF_WIDTH = 5.5
ONE_HOP = 1.125
THREE_HOP = -1.0 / 24.0
SITES = 196608.0

ZP, ZM, PK, SKL, SUB, DSK, DSKS, CC, CT1, CT3, CZ1, CZ3, ZZ, EX, SLOTS = (
    0, 1, 2, 4, 5, 6, 7, 8, 10, 12, 14, 16, 18, 26, 28)


def lanes(v, idx):
    return jnp.take_along_axis(v, idx, axis=1, mode="promise_in_bounds")


def rows(v, idx):
    return jnp.take_along_axis(v, idx, axis=0, mode="promise_in_bounds")


def tile_iota():
    row = lax.broadcasted_iota(jnp.int32, (8, 128), 0)
    lane = lax.broadcasted_iota(jnp.int32, (8, 128), 1)
    return row, lane


def mul_add(acc, links, field, back):
    out = []
    for a in range(3):
        total = acc[a]
        for b in range(3):
            total = total + links[b * 3 + a if back else a * 3 + b] * field[b]
        out.append(total)
    return out


def fill_positions(ix, t):
    row, lane = tile_iota()
    chunk = lane >> 4
    low = lane & 15
    zc = lane & 7
    ix[ZP] = (chunk << 4) | ((low + 1) & 15)
    ix[ZM] = (chunk << 4) | ((low - 1) & 15)
    ysrc = (chunk - t) & 7
    for par in range(2):
        ix[PK + par] = (ysrc << 4) | (zc << 1) | ((t + par + ysrc) & 1)
    ix[SKL] = (((chunk - row) & 7) << 4) | low
    ix[SUB] = (chunk - row) & 7
    ix[DSK] = (((chunk + row) & 7) << 4) | low
    ix[DSKS] = (((chunk + row) & 7) << 4) | (low ^ 8)
    for rho in range(2):
        z = (zc << 1) | ((chunk + row + rho) & 1)
        ix[CC + rho] = (((chunk + row) & 7) << 4) | z
        ix[CT1 + rho] = (((chunk + row - 1) & 7) << 4) | z
        ix[CT3 + rho] = (((chunk + row - 3) & 7) << 4) | z
        ix[CZ1 + rho] = (((chunk + row) & 7) << 4) | ((z - 1) & 15)
        ix[CZ3 + rho] = (((chunk + row) & 7) << 4) | ((z - 3) & 15)
        for j, d in enumerate((1, -1, 3, -3)):
            ix[ZZ + rho * 4 + j] = (lane & 120) | (((z + d) & 15) >> 1)
    ix[EX] = (chunk << 4) | (low >> 1)
    ix[EX + 1] = (chunk << 4) | 8 | (low >> 1)


def kernel(start_ref, smear_ref, fat_ref, naik_ref, proj_ref, out_ref,
           raw, sraw, yy, sx, syz, hh, af, prod, fs, fr, lraw, tl, tx, tyh, ll,
           ee, hn, hp, h2, fp, fps, ix, cb, mom, gone, gslot, gtm, kone, kslot, sone, sslot, stm,
           in_sem, y_send, y_recv, sx_send, sx_recv, l_send, l_recv, l_own, lh_send, lh_recv,
           f_send, f_recv, f_own, dx_send, dx_recv, dy_send, dy_recv,
           c_send, c_recv, r_send, r_recv, t_send, t_recv):
    t = lax.axis_index("tm")
    s = lax.axis_index("space")
    core = s & 1
    chip = s >> 1
    nxt = (t, (s + 1) & 15)
    prv = (t, (s + 15) & 15)
    ynxt = ((t + 1) & 7, s)
    yprv = ((t + 7) & 7, s)
    partner = (t, s + 1 - 2 * core)
    chips = [(t, (s + 2 * j) & 15) for j in range(1, 8)]
    times = [((t + d) & 7, s) for d in range(1, 8)]

    def remote(src, dst, send, recv, dev):
        return pltpu.make_async_remote_copy(src, dst, send, recv, device_id=dev, device_id_type=MESH)

    load_start = pltpu.make_async_copy(start_ref, raw, in_sem.at[0])
    load_smear = pltpu.make_async_copy(smear_ref, sraw, in_sem.at[1])
    load_start.start()
    load_smear.start()
    own_links = [
        pltpu.make_async_copy(ref.at[:, pl.ds(0, 6), t], lraw.at[t, i], l_own.at[i])
        for i, ref in enumerate((fat_ref, naik_ref))
    ]
    for c in own_links:
        c.start()

    barrier = pltpu.get_barrier_semaphore()
    friends = [nxt, prv] + chips + times
    for dev in friends:
        pl.semaphore_signal(barrier, inc=1, device_id=dev, device_id_type=MESH)

    fill_positions(ix, t)
    row, lane = tile_iota()
    high_half = (lane & 8) != 0

    load_start.wait()

    def place_start(i, _):
        for x in range(4):
            yy[0, 1 + x, i] = raw[pl.ds(i * 32 + x, 8, stride=4), :]
        return 0

    lax.fori_loop(0, 48, place_start, 0, unroll=4)
    pl.semaphore_wait(barrier, len(friends))

    def halo(n):
        return [
            remote(yy.at[n, 4], yy.at[n, 0], y_send.at[n, 0], y_recv.at[n, 0], nxt),
            remote(yy.at[n, 1], yy.at[n, 5], y_send.at[n, 1], y_recv.at[n, 1], prv),
        ]

    halos = halo(0)
    for c in halos:
        c.start()

    load_smear.wait()

    def ahead_y(v):
        r = pltpu.roll(v, 112, 1)
        return jnp.where(lane < 112, r, pltpu.roll(r, 7, 0))

    def behind_y(v):
        r = pltpu.roll(v, 16, 1)
        return jnp.where(lane >= 16, r, pltpu.roll(r, 1, 0))

    zp_i = ix[ZP]
    zm_i = ix[ZM]

    def place_smear(i, _):
        for x in range(4):
            sx[1 + x, i] = sraw[pl.ds(i * 32 + x, 8, stride=4), :]
            ly = sraw[pl.ds((9 + i) * 32 + x, 8, stride=4), :]
            lz = sraw[pl.ds((18 + i) * 32 + x, 8, stride=4), :]
            syz[x, 0, i] = ly
            syz[x, 1, i] = behind_y(ly)
            syz[x, 2, i] = lz
            syz[x, 3, i] = lanes(lz, zm_i)
        return 0

    lax.fori_loop(0, 9, place_smear, 0)
    sx_copy = remote(sx.at[4], sx.at[0], sx_send, sx_recv, nxt)
    sx_copy.start()

    link_copies = []
    for d in range(1, 8):
        dest = (t + d) & 7
        for i, ref in enumerate((fat_ref, naik_ref)):
            c = remote(ref.at[:, pl.ds(0, 6), dest], lraw.at[t, i],
                       l_send.at[i, d - 1], l_recv.at[i, d - 1], (dest, s))
            c.start()
            link_copies.append(c)

    def local_pass(n):
        def step(i, _):
            x = i >> 2
            base = (i & 3) * 12
            field = [[yy[n, 1 + x, base + v * 3 + c] for c in range(3)] for v in range(4)]
            acc = [[jnp.zeros((8, 128), F32)] * 3 for _ in range(4)]
            for d in range(4):
                links = [syz[x, d, e] for e in range(9)]
                for v in range(4):
                    if d == 0:
                        moved = [ahead_y(f) for f in field[v]]
                    elif d == 1:
                        moved = [behind_y(f) for f in field[v]]
                    else:
                        moved = [lanes(f, zp_i if d == 2 else zm_i) for f in field[v]]
                    acc[v] = mul_add(acc[v], links, moved, d & 1)
            for v in range(4):
                for c in range(3):
                    hh[x, base + v * 3 + c] = acc[v][c]
            return 0

        lax.fori_loop(0, 16, step, 0)

    def x_pass(n, plane_of, count, finish):
        def step(i, _):
            x = plane_of(i >> 2)
            base = (i & 3) * 12
            for back in (False, True):
                links = [sx[x if back else 1 + x, e] for e in range(9)]
                for v in range(4):
                    field = [yy[n, x if back else 2 + x, base + v * 3 + c] for c in range(3)]
                    acc = [hh[x, base + v * 3 + c] for c in range(3)] if not back else keep[v]
                    acc = mul_add(acc, links, field, back)
                    if not back:
                        if v == 0:
                            keep = []
                        keep.append(acc)
                    else:
                        for c in range(3):
                            finish(x, base + v * 3 + c, acc[c])
            return 0

        lax.fori_loop(0, 4 * count, step, 0)

    lflat = lraw.reshape(8 * 192, 128)

    def place_links(i, _):
        kind = i >> 2
        mu = i & 3
        for x in range(4):
            tiles = []
            for e in range(6):
                v = lanes(lflat[pl.ds(i * 24 + e * 4 + x, 8, stride=192), :], ix[SKL])
                tiles.append(rows(v, ix[SUB]))
            for a in range(3):
                b, c = (a + 1) % 3, (a + 2) % 3
                tiles.append(tiles[b] * tiles[3 + c] - tiles[c] * tiles[3 + b])
            for e in range(9):
                tl[x, kind, mu, e] = tiles[e]
        return 0

    for n in range(3):
        local_pass(n)
        if n == 0:
            sx_copy.wait()
        if n == 2:
            for c in own_links + link_copies:
                c.wait()
            lax.fori_loop(0, 8, place_links, 0)
            link_halos = [
                remote(tl.at[3, 0, 0], tx.at[0, 3], lh_send.at[0, 0], lh_recv.at[0, 0], nxt),
                remote(tl.at[pl.ds(1, 3), 1, 0], tx.at[1, pl.ds(1, 3)], lh_send.at[0, 1], lh_recv.at[0, 1], nxt),
                remote(tl.at[:, 0, 1, :, pl.ds(7, 1)], tyh.at[0, :, :, pl.ds(7, 1)],
                       lh_send.at[1, 0], lh_recv.at[1, 0], ynxt),
                remote(tl.at[:, 1, 1, :, pl.ds(5, 3)], tyh.at[1, :, :, pl.ds(5, 3)],
                       lh_send.at[1, 1], lh_recv.at[1, 1], ynxt),
            ]
        for c in halos:
            c.wait()

        def finish(x, comp, acc, n=n):
            if n == 0:
                value = (-0.5 / HALF_WIDTH) * yy[0, 1 + x, comp] - (1.0 / HALF_WIDTH) * acc
            else:
                value = ((-1.0 / HALF_WIDTH) * yy[n, 1 + x, comp] - (2.0 / HALF_WIDTH) * acc
                         - yy[n - 1, 1 + x, comp])
            yy[n + 1, 1 + x, comp] = value

        x_pass(n, lambda i: 3 * i, 2, finish)
        if n < 2:
            halos = halo(n + 1)
            for c in halos:
                c.start()
        if n == 2:
            for c in link_halos:
                c.start()
        x_pass(n, lambda i: 1 + i, 2, finish)

    def products(left, right):
        def step(k, _):
            mine = [left(x, k * 3 + c) for x in range(4) for c in range(3)]
            for d in range(9):
                j = (k + d) & 15
                total = None
                for x in range(4):
                    for c in range(3):
                        term = mine[x * 3 + c] * right(x, j * 3 + c)
                        total = term if total is None else total + term
                total = jnp.sum(total, axis=0, keepdims=True)
                prod[pl.ds(j * 16 + k, 1), :] = total
                prod[pl.ds(k * 16 + j, 1), :] = total
            return 0

        lax.fori_loop(0, 16, step, 0)
        sums = lax.dot_general(jnp.ones((8, 128), F32), prod[...], (((1,), (1,)), ((), ())),
                               precision=HIGH, preferred_element_type=F32)
        return jnp.where(row == 0, sums[:, :128], sums[:, 128:])

    def to_partner(buf, which):
        return remote(buf.at[0], buf.at[1], c_send.at[which], c_recv.at[which], partner)

    def to_chips(buf, which):
        return [remote(buf.at[chip], buf.at[chip], r_send.at[which, j], r_recv.at[which, j], chips[j])
                for j in range(7)]

    def to_times(buf, which):
        return [remote(buf.at[t], buf.at[t], t_send.at[which, j], t_recv.at[which, j], times[j])
                for j in range(7)]

    def total_of(buf):
        total = buf[0]
        for j in range(1, 8):
            total = total + buf[j]
        return total

    gone[0] = products(lambda x, e: yy[3, 1 + x, e], lambda x, e: yy[3, 1 + x, e])
    g_partner = to_partner(gone, 0)
    g_partner.start()
    def pack(i, _):
        x = i >> 3
        pair = i & 7
        idx = ix[PK + (x & 1)]
        for c in range(3):
            one = lanes(yy[3, 1 + x, pair * 3 + c], idx)
            two = lanes(yy[3, 1 + x, pair * 3 + 24 + c], idx)
            fs[pl.ds(x * 24 + pair * 3 + c, 8, stride=96), :] = jnp.where(high_half, two, one)
        return 0

    lax.fori_loop(0, 32, pack, 0)

    def part(ref, which):
        return ref.at[pl.ds(pl.multiple_of(which * 96, 96), 96)]

    f_copies = [
        remote(part(fs, (t + d) & 7), part(fr, t), f_send.at[d - 1], f_recv.at[d - 1], times[d - 1])
        for d in range(1, 8)
    ]
    for c in f_copies:
        c.start()
    f_local = pltpu.make_async_copy(part(fs, t), part(fr, t), f_own)
    f_local.start()

    g_partner.wait()
    gslot[chip] = gone[0] + gone[1]
    g_chips = to_chips(gslot, 0)
    for c in g_chips:
        c.start()

    halos = halo(3)
    for c in halos:
        c.start()
    for c in link_halos:
        c.wait()

    chunk = lane >> 4

    def fill_links(i, _):
        x = i & 3
        e = i >> 2
        xsign = (1 - 2 * (x & 1)).astype(F32)
        ysign = (1 - 2 * (row & 1)).astype(F32)
        tsign = (1 - 2 * (chunk & 1)).astype(F32)
        for kind, hop, weight in ((0, 1, 0.5 * ONE_HOP), (1, 3, 0.5 * THREE_HOP)):
            px = x - hop
            own = [tl[x, kind, mu, e] for mu in range(4)]
            before_x = jnp.where(px >= 0, tl[jnp.maximum(px, 0), kind, 0, e],
                                 tx[kind, jnp.minimum(px + 4, 3), e])
            before_y = pltpu.roll(jnp.where(row < 8 - hop, own[1], tyh[kind, x, e]), hop, 0)
            for pi in range(2):
                rho = (x + pi) & 1
                cc = ix[CC + rho]
                ct = ix[(CT3 if kind else CT1) + rho]
                cz = ix[(CZ3 if kind else CZ1) + rho]
                pis = -1.0 if pi else 1.0
                scale = [
                    jnp.full((8, 128), weight, F32),
                    jnp.full((8, 128), weight, F32) * xsign,
                    weight * xsign * ysign,
                ]
                fwd = [lanes(own[mu], cc) for mu in range(4)]
                bwd = [lanes(before_x, cc), lanes(before_y, ct), lanes(own[2], cz), lanes(own[3], ct)]
                for mu in range(4):
                    if mu < 3:
                        up, down = scale[mu], -scale[mu]
                    else:
                        up = jnp.where(chunk < 8 - hop, (pis * weight) * tsign, 0.0)
                        down = jnp.where(chunk >= hop, (-pis * weight) * tsign, 0.0)
                    ll[pi, x, (mu * 2 + kind) * 2, e] = up * fwd[mu]
                    ll[pi, x, (mu * 2 + kind) * 2 + 1, e] = down * bwd[mu]
        return 0

    lax.fori_loop(0, 36, fill_links, 0)

    for c in g_chips:
        c.wait()
    gtm[t] = total_of(gslot)
    g_times = to_times(gtm, 0)
    for c in g_times:
        c.start()

    for c in f_copies:
        c.wait()
    f_local.wait()

    def unpack(i, _):
        x = i >> 1
        for c in range(12):
            e = (i & 1) * 12 + c
            v = rows(fr[pl.ds(x * 24 + e, 8, stride=96), :], ix[SUB])
            fp[x, e] = lanes(v, ix[DSK])
            fps[x, e] = lanes(v, ix[DSKS])
        return 0

    lax.fori_loop(0, 8, unpack, 0)

    for c in g_times:
        c.wait()

    flat = gtm.reshape(64, 128)
    for half in range(2):
        cb[pl.ds(128 * half, 128), :] = lax.dot_general(
            flat[pl.ds(half, 8, stride=8), :], jnp.where(chunk == row, 1.0, 0.0).astype(F32),
            (((0,), (0,)), ((), ())), precision=HIGH, preferred_element_type=F32)
    cols = [cb[pl.ds(16 * m, 16), :] * (1.0 / SITES) for m in range(16)]
    line = lax.broadcasted_iota(jnp.int32, (16, 128), 0)
    inv = [jnp.where(line == m, 1.0, 0.0).astype(F32) for m in range(16)]
    for j in range(16):
        scale = 1.0 / jnp.sqrt(cols[j][j:j + 1])
        factor = jnp.where(line > j, cols[j] * scale, 0.0)
        for m in range(j + 1, 16):
            cols[m] = cols[m] - factor * (cols[m][j:j + 1] * scale)
        for m in range(j + 1):
            top = inv[m][j:j + 1] * scale
            inv[m] = jnp.where(line == j, top, inv[m] - factor * top)
    for m in range(16):
        cb[pl.ds(16 * m, 16), :] = inv[m]

    def entry(k, j):
        return jnp.broadcast_to(cb[pl.ds(16 * j + k, 1), :], (8, 128))

    for pair in range(8):
        same = [jnp.where(high_half, entry(pair + 8, j + 8), entry(pair, j)) for j in range(pair + 1)]
        cross = [jnp.where(high_half, entry(pair + 8, j), 0.0) for j in range(8)]

        def mix(x, total, pair=pair, same=same, cross=cross):
            for c in range(3):
                value = cross[0] * fps[x, c]
                for j in range(1, 8):
                    value = value + cross[j] * fps[x, j * 3 + c]
                for j in range(pair + 1):
                    value = value + same[j] * fp[x, j * 3 + c]
                ee[0, 3 + x, pair * 3 + c] = value
                total = total + value * value
            return total

        mom[0, pair] = lax.fori_loop(0, 4, mix, jnp.zeros((8, 128), F32))

    def d_halo(n):
        return [
            remote(ee.at[n, pl.ds(4, 3)], ee.at[n, pl.ds(0, 3)], dx_send.at[n, 0], dx_recv.at[n, 0], nxt),
            remote(ee.at[n, pl.ds(3, 3)], ee.at[n, pl.ds(7, 3)], dx_send.at[n, 1], dx_recv.at[n, 1], prv),
            remote(ee.at[n, pl.ds(3, 4), :, pl.ds(5, 3)], hp.at[n, :, :, pl.ds(5, 3)],
                   dy_send.at[n, 0], dy_recv.at[n, 0], ynxt),
            remote(ee.at[n, pl.ds(3, 4), :, pl.ds(0, 3)], hn.at[n, :, :, pl.ds(0, 3)],
                   dy_send.at[n, 1], dy_recv.at[n, 1], yprv),
        ]

    def inner_pass(n, pi):
        def step(i, _):
            x = i >> 1
            base = (i & 1) * 12
            rho = (x + pi) & 1
            field = [[ee[n, 3 + x, base + v * 3 + c] for c in range(3)] for v in range(4)]
            acc = [[jnp.zeros((8, 128), F32)] * 3 for _ in range(4)]
            for d in range(8, 16):
                links = [ll[pi, x, d, e] for e in range(9)]
                hop = 3 if (d >> 1) & 1 else 1
                if d < 12:
                    idx = ix[ZZ + rho * 4 + (d - 8)]
                for v in range(4):
                    if d < 12:
                        moved = [lanes(f, idx) for f in field[v]]
                    else:
                        shift = 16 * hop if d & 1 else 128 - 16 * hop
                        moved = [pltpu.roll(f, shift, 1) for f in field[v]]
                    acc[v] = mul_add(acc[v], links, moved, d & 1)
            for v in range(4):
                for c in range(3):
                    h2[x, base + v * 3 + c] = acc[v][c]
            return 0

        lax.fori_loop(0, 8, step, 0)

    def outer_pass(n, pi, store):
        for pair in range(8):
            mom[n + 1, pair] = jnp.zeros((8, 128), F32)

        def step(i, _):
            x = i >> 1
            base = (i & 1) * 12
            acc = [[h2[x, base + v * 3 + c] for c in range(3)] for v in range(4)]
            for d in range(8):
                links = [ll[pi, x, d, e] for e in range(9)]
                hop = 3 if (d >> 1) & 1 else 1
                for v in range(4):
                    comps = [base + v * 3 + c for c in range(3)]
                    if d < 4:
                        moved = [ee[n, 3 + x - hop if d & 1 else 3 + x + hop, e] for e in comps]
                    elif d & 1:
                        moved = [pltpu.roll(jnp.where(row < 8 - hop, ee[n, 3 + x, e], hp[n, x, e]), hop, 0)
                                 for e in comps]
                    else:
                        moved = [pltpu.roll(jnp.where(row >= hop, ee[n, 3 + x, e], hn[n, x, e]), 8 - hop, 0)
                                 for e in comps]
                    acc[v] = mul_add(acc[v], links, moved, d & 1)
            for v in range(4):
                for c in range(3):
                    if store:
                        ee[n + 1, 3 + x, base + v * 3 + c] = acc[v][c]
                mom[n + 1, (i & 1) * 4 + v] += (
                    acc[v][0] * acc[v][0] + acc[v][1] * acc[v][1] + acc[v][2] * acc[v][2])
            return 0

        lax.fori_loop(0, 8, step, 0)

    def flat_to_square(tile):
        total = jnp.zeros((16, 128), F32)
        for m in range(16):
            piece = jnp.broadcast_to(tile[m >> 3:(m >> 3) + 1], (16, 128))
            piece = pltpu.roll(piece, (128 - 16 * (m & 7)) & 127, 1) if m & 7 else piece
            total = jnp.where(line == m, piece, total)
        return total[:, :16]

    for n in range(3):
        pi = 1 - (n & 1)
        d_copies = d_halo(n)
        for c in d_copies:
            c.start()
        inner_pass(n, pi)
        if n == 0:
            local_pass(3)
            for c in halos:
                c.wait()

            def keep_image(x, comp, acc):
                af[x, comp] = 6.0 * yy[3, 1 + x, comp] - acc

            x_pass(3, lambda i: i, 4, keep_image)
            kone[0] = products(lambda x, e: yy[3, 1 + x, e], lambda x, e: af[x, e])
            k_partner = to_partner(kone, 1)
            k_partner.start()
        if n == 1:
            k_partner.wait()
            kslot[chip] = kone[0] + kone[1]
            k_chips = to_chips(kslot, 1)
            for c in k_chips:
                c.start()
        if n == 2:
            for c in k_chips:
                c.wait()
            square = flat_to_square(total_of(kslot))
            pick = jnp.where(lane == t * 16, 1.0, 0.0).astype(F32)
            weights = lax.dot_general(pick, cb[...], (((1,), (1,)), ((), ())),
                                      precision=HIGH, preferred_element_type=F32)
            weights = flat_to_square(jnp.where(row == 0, weights[:, :128], weights[:, 128:]))
            half = lax.dot_general(weights, square, (((0,), (0,)), ((), ())),
                                   precision=HIGH, preferred_element_type=F32)
            proj_ref[0] = lax.dot_general(half, weights, (((1,), (0,)), ((), ())),
                                          precision=HIGH, preferred_element_type=F32)
        for c in d_copies:
            c.wait()
        outer_pass(n, pi, n < 2)

    prod[...] = jnp.zeros((256, 128), F32)
    for m in range(4):
        for pair in range(8):
            prod[pl.ds(8 * m + pair, 1), :] = jnp.sum(mom[m, pair], axis=0, keepdims=True)
    select = jnp.where(((lane >> 3) & 1) == row, 1.0, 0.0).astype(F32)
    sone[0] = lax.dot_general(select, prod[pl.ds(0, 128), :], (((1,), (1,)), ((), ())),
                              precision=HIGH, preferred_element_type=F32)
    s_partner = to_partner(sone, 2)
    s_partner.start()
    s_partner.wait()
    sslot[chip] = sone[0] + sone[1]
    s_chips = to_chips(sslot, 2)
    for c in s_chips:
        c.start()
    for c in s_chips:
        c.wait()
    stm[t] = total_of(sslot)
    s_times = to_times(stm, 1)
    for c in s_times:
        c.start()
    for c in s_times:
        c.wait()
    n0 = total_of(stm)
    n1 = pltpu.roll(n0, 120, 1)
    n2 = pltpu.roll(n0, 112, 1)
    n3 = pltpu.roll(n0, 104, 1)
    ratio = n1 / n0
    alpha0 = 1.0 / (0.25 + ratio)
    rr = alpha0 * alpha0 * (n2 - ratio * n1)
    beta = rr / n0
    a = alpha0 * ratio + beta
    energy = 0.25 * rr * (1.0 + beta) + a * a * n1 - 2.0 * a * alpha0 * n2 + alpha0 * alpha0 * n3
    alpha1 = rr / energy
    first = alpha0 + alpha1 * a
    second = alpha1 * alpha0

    def spread(v, pair):
        low = jnp.broadcast_to(v[0:1, pair:pair + 1], (8, 128))
        high = jnp.broadcast_to(v[1:2, pair:pair + 1], (8, 128))
        return jnp.where(high_half, high, low)

    for pair in range(8):
        ca = spread(first, pair)
        cd = spread(second, pair)

        def finish_out(x, _, pair=pair, ca=ca, cd=cd):
            for c in range(3):
                value = ca * ee[0, 3 + x, pair * 3 + c] + cd * ee[2, 3 + x, pair * 3 + c]
                out_ref[pair, c, x] = lanes(value, ix[EX])
                out_ref[pair + 8, c, x] = lanes(value, ix[EX + 1])
            return 0

        lax.fori_loop(0, 4, finish_out, 0, unroll=True)


def rows_first(array, lead):
    return array.reshape(lead, 4, 8, 128).transpose(0, 2, 1, 3)


def body(start, smear_links, fat_links, naik_links):
    start = rows_first(start, 48).reshape(1536, 128)
    smear = rows_first(smear_links, 27).reshape(864, 128)
    fat = rows_first(fat_links, 36).reshape(4, 9, 8, 4, 128)
    naik = rows_first(naik_links, 36).reshape(4, 9, 8, 4, 128)
    vm = lambda *shape: pltpu.VMEM(shape, F32)
    dma = lambda *shape: pltpu.SemaphoreType.DMA(shape) if shape else pltpu.SemaphoreType.DMA
    anywhere = pl.BlockSpec(memory_space=pl.ANY)
    local = pl.BlockSpec(memory_space=pltpu.VMEM)
    projected, filled = pl.pallas_call(
        kernel,
        out_shape=(jax.ShapeDtypeStruct((1, 16, 16), F32),
                   jax.ShapeDtypeStruct((16, 3, 4, 8, 128), F32)),
        in_specs=[anywhere] * 4,
        out_specs=(local, local),
        scratch_shapes=[
            vm(1536, 128), vm(864, 128), vm(4, 6, 48, 8, 128), vm(5, 9, 8, 128), vm(4, 4, 9, 8, 128),
            vm(4, 48, 8, 128), vm(4, 48, 8, 128), vm(256, 128), vm(768, 128), vm(768, 128),
            vm(8, 2, 4, 6, 4, 128),
            vm(4, 2, 4, 9, 8, 128), vm(2, 4, 9, 8, 128), vm(2, 4, 9, 8, 128), vm(2, 4, 16, 9, 8, 128),
            vm(3, 10, 24, 8, 128), vm(3, 4, 24, 8, 128), vm(3, 4, 24, 8, 128), vm(4, 24, 8, 128),
            vm(4, 24, 8, 128), vm(4, 24, 8, 128), pltpu.VMEM((SLOTS, 8, 128), jnp.int32),
            vm(256, 128), vm(4, 8, 8, 128),
            vm(2, 8, 128), vm(8, 8, 128), vm(8, 8, 128),
            vm(2, 8, 128), vm(8, 8, 128),
            vm(2, 8, 128), vm(8, 8, 128), vm(8, 8, 128),
            dma(2), dma(4, 2), dma(4, 2), dma(), dma(), dma(2, 7), dma(2, 7), dma(2),
            dma(2, 2), dma(2, 2), dma(7), dma(7), dma(),
            dma(3, 2), dma(3, 2), dma(3, 2), dma(3, 2),
            dma(3), dma(3), dma(3, 7), dma(3, 7), dma(2, 7), dma(2, 7),
        ],
        compiler_params=pltpu.CompilerParams(
            collective_id=0, has_side_effects=True, vmem_limit_bytes=60 * 2**20),
        name="distill",
    )(start, smear, fat, naik)
    place = [lax.broadcasted_iota(jnp.int32, (4, 8, 128), d) for d in range(3)]
    even = ((place[0] + place[1] + (place[2] >> 4) + place[2]) & 1) == 0
    return projected * (1.0 / SITES), jnp.where(even, filled, 0.0)


def solution(mesh):
    in_specs = (
        P(None, None, "tm", "space", None),
        P(None, None, None, "tm", "space", None),
        P(None, None, None, "tm", "space", None),
        P(None, None, None, "tm", "space", None),
    )
    out_specs = (P("tm", None, None), P(None, None, "space", "tm", None))
    return jax.shard_map(body, mesh=mesh, in_specs=in_specs, out_specs=out_specs, check_vma=False)
```

```python
import functools
import jax
import jax.numpy as jnp
from jax import lax
from jax.sharding import PartitionSpec as P
import jax.experimental.pallas as pl
import jax.experimental.pallas.tpu as pltpu

MESH = pl.DeviceIdType.MESH
HIGH = lax.Precision.HIGHEST
F32 = jnp.float32
CENTER = 6.5
HALF_WIDTH = 5.5
ONE_HOP = 1.125
THREE_HOP = -1.0 / 24.0
SITES = 196608.0

ZP, ZM, PK, SKL, SUB, DSK, DSKS, CC, CT1, CT3, CZ1, CZ3, ZZ, EX, SLOTS = (
    0, 1, 2, 4, 5, 6, 7, 8, 10, 12, 14, 16, 18, 26, 28)


def lanes(v, idx):
    return jnp.take_along_axis(v, idx, axis=1, mode="promise_in_bounds")


def rows(v, idx):
    return jnp.take_along_axis(v, idx, axis=0, mode="promise_in_bounds")


def tile_iota():
    row = lax.broadcasted_iota(jnp.int32, (8, 128), 0)
    lane = lax.broadcasted_iota(jnp.int32, (8, 128), 1)
    return row, lane


def mul_add(acc, links, field, back):
    out = []
    for a in range(3):
        total = acc[a]
        for b in range(3):
            total = total + links[b * 3 + a if back else a * 3 + b] * field[b]
        out.append(total)
    return out


def fill_positions(ix, t):
    row, lane = tile_iota()
    chunk = lane >> 4
    low = lane & 15
    zc = lane & 7
    ix[ZP] = (chunk << 4) | ((low + 1) & 15)
    ix[ZM] = (chunk << 4) | ((low - 1) & 15)
    ysrc = (chunk - t) & 7
    for par in range(2):
        ix[PK + par] = (ysrc << 4) | (zc << 1) | ((t + par + ysrc) & 1)
    ix[SKL] = (((chunk - row) & 7) << 4) | low
    ix[SUB] = (chunk - row) & 7
    ix[DSK] = (((chunk + row) & 7) << 4) | low
    ix[DSKS] = (((chunk + row) & 7) << 4) | (low ^ 8)
    for rho in range(2):
        z = (zc << 1) | ((chunk + row + rho) & 1)
        ix[CC + rho] = (((chunk + row) & 7) << 4) | z
        ix[CT1 + rho] = (((chunk + row - 1) & 7) << 4) | z
        ix[CT3 + rho] = (((chunk + row - 3) & 7) << 4) | z
        ix[CZ1 + rho] = (((chunk + row) & 7) << 4) | ((z - 1) & 15)
        ix[CZ3 + rho] = (((chunk + row) & 7) << 4) | ((z - 3) & 15)
        for j, d in enumerate((1, -1, 3, -3)):
            ix[ZZ + rho * 4 + j] = (lane & 120) | (((z + d) & 15) >> 1)
    ix[EX] = (chunk << 4) | (low >> 1)
    ix[EX + 1] = (chunk << 4) | 8 | (low >> 1)


def kernel(start_ref, smear_ref, fat_ref, naik_ref, proj_ref, out_ref,
           raw, sraw, yy, sx, syz, hh, af, prod, fs, fr, lraw, tl, tx, tyh, ll,
           ee, hn, hp, h2, fp, fps, ix, cb, mom, gone, gslot, gtm, kone, kslot, sone, sslot, stm,
           in_sem, y_send, y_recv, sx_send, sx_recv, l_send, l_recv, l_own, lh_send, lh_recv,
           f_send, f_recv, f_own, dx_send, dx_recv, dy_send, dy_recv,
           c_send, c_recv, r_send, r_recv, t_send, t_recv):
    t = lax.axis_index("tm")
    s = lax.axis_index("space")
    core = s & 1
    chip = s >> 1
    nxt = (t, (s + 1) & 15)
    prv = (t, (s + 15) & 15)
    ynxt = ((t + 1) & 7, s)
    yprv = ((t + 7) & 7, s)
    partner = (t, s + 1 - 2 * core)
    chips = [(t, (s + 2 * j) & 15) for j in range(1, 8)]
    times = [((t + d) & 7, s) for d in range(1, 8)]

    def remote(src, dst, send, recv, dev):
        return pltpu.make_async_remote_copy(src, dst, send, recv, device_id=dev, device_id_type=MESH)

    load_start = pltpu.make_async_copy(start_ref, raw, in_sem.at[0])
    load_smear = pltpu.make_async_copy(smear_ref, sraw, in_sem.at[1])
    load_start.start()
    load_smear.start()
    own_links = [
        pltpu.make_async_copy(ref.at[:, pl.ds(0, 6), t], lraw.at[t, i], l_own.at[i])
        for i, ref in enumerate((fat_ref, naik_ref))
    ]
    for c in own_links:
        c.start()

    barrier = pltpu.get_barrier_semaphore()
    friends = [nxt, prv] + chips + times
    for dev in friends:
        pl.semaphore_signal(barrier, inc=1, device_id=dev, device_id_type=MESH)

    fill_positions(ix, t)
    row, lane = tile_iota()
    high_half = (lane & 8) != 0

    load_start.wait()

    def place_start(i, _):
        for x in range(4):
            yy[0, 1 + x, i] = raw[pl.ds(i * 32 + x, 8, stride=4), :]
        return 0

    lax.fori_loop(0, 48, place_start, 0, unroll=4)
    pl.semaphore_wait(barrier, len(friends))

    def halo(n, h):
        part = pl.ds(24 * h, 24)
        return [
            remote(yy.at[n, 4, part], yy.at[n, 0, part], y_send.at[n, h, 0], y_recv.at[n, h, 0], nxt),
            remote(yy.at[n, 1, part], yy.at[n, 5, part], y_send.at[n, h, 1], y_recv.at[n, h, 1], prv),
        ]

    def begin(copies):
        for c in copies:
            c.start()
        return copies

    def end(copies):
        for c in copies:
            c.wait()

    halos = [begin(halo(0, h)) for h in range(2)]

    load_smear.wait()

    def ahead_y(v):
        r = pltpu.roll(v, 112, 1)
        return jnp.where(lane < 112, r, pltpu.roll(r, 7, 0))

    def behind_y(v):
        r = pltpu.roll(v, 16, 1)
        return jnp.where(lane >= 16, r, pltpu.roll(r, 1, 0))

    zp_i = ix[ZP]
    zm_i = ix[ZM]

    def place_smear(i, _):
        for x in range(4):
            sx[1 + x, i] = sraw[pl.ds(i * 32 + x, 8, stride=4), :]
            ly = sraw[pl.ds((9 + i) * 32 + x, 8, stride=4), :]
            lz = sraw[pl.ds((18 + i) * 32 + x, 8, stride=4), :]
            syz[x, 0, i] = ly
            syz[x, 1, i] = behind_y(ly)
            syz[x, 2, i] = lz
            syz[x, 3, i] = lanes(lz, zm_i)
        return 0

    lax.fori_loop(0, 9, place_smear, 0)
    sx_copy = remote(sx.at[4], sx.at[0], sx_send, sx_recv, nxt)
    sx_copy.start()

    link_copies = []
    for d in range(1, 8):
        dest = (t + d) & 7
        for i, ref in enumerate((fat_ref, naik_ref)):
            c = remote(ref.at[:, pl.ds(0, 6), dest], lraw.at[t, i],
                       l_send.at[i, d - 1], l_recv.at[i, d - 1], (dest, s))
            c.start()
            link_copies.append(c)

    def local_pass(n, h):
        def step(i, _):
            x = i >> 1
            base = 24 * h + (i & 1) * 12
            field = [[yy[n, 1 + x, base + v * 3 + c] for c in range(3)] for v in range(4)]
            acc = [[jnp.zeros((8, 128), F32)] * 3 for _ in range(4)]
            for d in range(4):
                links = [syz[x, d, e] for e in range(9)]
                for v in range(4):
                    if d == 0:
                        moved = [ahead_y(f) for f in field[v]]
                    elif d == 1:
                        moved = [behind_y(f) for f in field[v]]
                    else:
                        moved = [lanes(f, zp_i if d == 2 else zm_i) for f in field[v]]
                    acc[v] = mul_add(acc[v], links, moved, d & 1)
            for v in range(4):
                for c in range(3):
                    hh[x, base + v * 3 + c] = acc[v][c]
            return 0

        lax.fori_loop(0, 8, step, 0)

    def x_pass(n, h, plane_of, count, finish):
        def step(i, _):
            x = plane_of(i >> 1)
            base = 24 * h + (i & 1) * 12
            for back in (False, True):
                links = [sx[x if back else 1 + x, e] for e in range(9)]
                for v in range(4):
                    field = [yy[n, x if back else 2 + x, base + v * 3 + c] for c in range(3)]
                    acc = [hh[x, base + v * 3 + c] for c in range(3)] if not back else keep[v]
                    acc = mul_add(acc, links, field, back)
                    if not back:
                        if v == 0:
                            keep = []
                        keep.append(acc)
                    else:
                        for c in range(3):
                            finish(x, base + v * 3 + c, acc[c])
            return 0

        lax.fori_loop(0, 2 * count, step, 0)

    lflat = lraw.reshape(8 * 192, 128)

    def place_links(i, _):
        kind = i >> 2
        mu = i & 3
        for x in range(4):
            tiles = []
            for e in range(6):
                v = lanes(lflat[pl.ds(i * 24 + e * 4 + x, 8, stride=192), :], ix[SKL])
                tiles.append(rows(v, ix[SUB]))
            for a in range(3):
                b, c = (a + 1) % 3, (a + 2) % 3
                tiles.append(tiles[b] * tiles[3 + c] - tiles[c] * tiles[3 + b])
            for e in range(9):
                tl[x, kind, mu, e] = tiles[e]
        return 0

    for n in range(3):
        for h in range(2):
            local_pass(n, h)
            if n == 0 and h == 0:
                sx_copy.wait()
            if n == 2 and h == 0:
                for c in own_links + link_copies:
                    c.wait()
                lax.fori_loop(0, 8, place_links, 0)
                link_halos = [
                    remote(tl.at[3, 0, 0], tx.at[0, 3], lh_send.at[0, 0], lh_recv.at[0, 0], nxt),
                    remote(tl.at[pl.ds(1, 3), 1, 0], tx.at[1, pl.ds(1, 3)], lh_send.at[0, 1], lh_recv.at[0, 1], nxt),
                    remote(tl.at[:, 0, 1, :, pl.ds(7, 1)], tyh.at[0, :, :, pl.ds(7, 1)],
                           lh_send.at[1, 0], lh_recv.at[1, 0], ynxt),
                    remote(tl.at[:, 1, 1, :, pl.ds(5, 3)], tyh.at[1, :, :, pl.ds(5, 3)],
                           lh_send.at[1, 1], lh_recv.at[1, 1], ynxt),
                ]
            end(halos[h])

            def finish(x, comp, acc, n=n):
                if n == 0:
                    value = (-0.5 / HALF_WIDTH) * yy[0, 1 + x, comp] - (1.0 / HALF_WIDTH) * acc
                else:
                    value = ((-1.0 / HALF_WIDTH) * yy[n, 1 + x, comp] - (2.0 / HALF_WIDTH) * acc
                             - yy[n - 1, 1 + x, comp])
                yy[n + 1, 1 + x, comp] = value

            x_pass(n, h, lambda i: 3 * i, 2, finish)
            if n < 2:
                halos[h] = begin(halo(n + 1, h))
            if n == 2 and h == 0:
                begin(link_halos)
            x_pass(n, h, lambda i: 1 + i, 2, finish)

    def products(left, right):
        def step(k, _):
            mine = [left(x, k * 3 + c) for x in range(4) for c in range(3)]
            for d in range(9):
                j = (k + d) & 15
                total = None
                for x in range(4):
                    for c in range(3):
                        term = mine[x * 3 + c] * right(x, j * 3 + c)
                        total = term if total is None else total + term
                total = jnp.sum(total, axis=0, keepdims=True)
                prod[pl.ds(j * 16 + k, 1), :] = total
                prod[pl.ds(k * 16 + j, 1), :] = total
            return 0

        lax.fori_loop(0, 16, step, 0)
        sums = lax.dot_general(jnp.ones((8, 128), F32), prod[...], (((1,), (1,)), ((), ())),
                               precision=HIGH, preferred_element_type=F32)
        return jnp.where(row == 0, sums[:, :128], sums[:, 128:])

    def to_partner(buf, which):
        return remote(buf.at[0], buf.at[1], c_send.at[which], c_recv.at[which], partner)

    def to_chips(buf, which):
        return [remote(buf.at[chip], buf.at[chip], r_send.at[which, j], r_recv.at[which, j], chips[j])
                for j in range(7)]

    def to_times(buf, which):
        return [remote(buf.at[t], buf.at[t], t_send.at[which, j], t_recv.at[which, j], times[j])
                for j in range(7)]

    def total_of(buf):
        total = buf[0]
        for j in range(1, 8):
            total = total + buf[j]
        return total

    gone[0] = products(lambda x, e: yy[3, 1 + x, e], lambda x, e: yy[3, 1 + x, e])
    g_partner = to_partner(gone, 0)
    g_partner.start()
    def pack(i, _):
        x = i >> 3
        pair = i & 7
        idx = ix[PK + (x & 1)]
        for c in range(3):
            one = lanes(yy[3, 1 + x, pair * 3 + c], idx)
            two = lanes(yy[3, 1 + x, pair * 3 + 24 + c], idx)
            fs[pl.ds(x * 24 + pair * 3 + c, 8, stride=96), :] = jnp.where(high_half, two, one)
        return 0

    lax.fori_loop(0, 32, pack, 0)

    def part(ref, which):
        return ref.at[pl.ds(pl.multiple_of(which * 96, 96), 96)]

    f_copies = [
        remote(part(fs, (t + d) & 7), part(fr, t), f_send.at[d - 1], f_recv.at[d - 1], times[d - 1])
        for d in range(1, 8)
    ]
    for c in f_copies:
        c.start()
    f_local = pltpu.make_async_copy(part(fs, t), part(fr, t), f_own)
    f_local.start()

    g_partner.wait()
    gslot[chip] = gone[0] + gone[1]
    g_chips = to_chips(gslot, 0)
    for c in g_chips:
        c.start()

    halos = [begin(halo(3, h)) for h in range(2)]
    for c in link_halos:
        c.wait()

    chunk = lane >> 4

    def fill_links(i, _):
        x = i & 3
        e = i >> 2
        xsign = (1 - 2 * (x & 1)).astype(F32)
        ysign = (1 - 2 * (row & 1)).astype(F32)
        tsign = (1 - 2 * (chunk & 1)).astype(F32)
        for kind, hop, weight in ((0, 1, 0.5 * ONE_HOP), (1, 3, 0.5 * THREE_HOP)):
            px = x - hop
            own = [tl[x, kind, mu, e] for mu in range(4)]
            before_x = jnp.where(px >= 0, tl[jnp.maximum(px, 0), kind, 0, e],
                                 tx[kind, jnp.minimum(px + 4, 3), e])
            before_y = pltpu.roll(jnp.where(row < 8 - hop, own[1], tyh[kind, x, e]), hop, 0)
            for pi in range(2):
                rho = (x + pi) & 1
                cc = ix[CC + rho]
                ct = ix[(CT3 if kind else CT1) + rho]
                cz = ix[(CZ3 if kind else CZ1) + rho]
                pis = -1.0 if pi else 1.0
                scale = [
                    jnp.full((8, 128), weight, F32),
                    jnp.full((8, 128), weight, F32) * xsign,
                    weight * xsign * ysign,
                ]
                fwd = [lanes(own[mu], cc) for mu in range(4)]
                bwd = [lanes(before_x, cc), lanes(before_y, ct), lanes(own[2], cz), lanes(own[3], ct)]
                for mu in range(4):
                    if mu < 3:
                        up, down = scale[mu], -scale[mu]
                    else:
                        up = jnp.where(chunk < 8 - hop, (pis * weight) * tsign, 0.0)
                        down = jnp.where(chunk >= hop, (-pis * weight) * tsign, 0.0)
                    ll[pi, x, (mu * 2 + kind) * 2, e] = up * fwd[mu]
                    ll[pi, x, (mu * 2 + kind) * 2 + 1, e] = down * bwd[mu]
        return 0

    lax.fori_loop(0, 36, fill_links, 0)

    for c in g_chips:
        c.wait()
    gtm[t] = total_of(gslot)
    g_times = to_times(gtm, 0)
    for c in g_times:
        c.start()

    for c in f_copies:
        c.wait()
    f_local.wait()

    def unpack(i, _):
        x = i >> 1
        for c in range(12):
            e = (i & 1) * 12 + c
            v = rows(fr[pl.ds(x * 24 + e, 8, stride=96), :], ix[SUB])
            fp[x, e] = lanes(v, ix[DSK])
            fps[x, e] = lanes(v, ix[DSKS])
        return 0

    lax.fori_loop(0, 8, unpack, 0)

    for c in g_times:
        c.wait()

    flat = gtm.reshape(64, 128)
    for half in range(2):
        cb[pl.ds(128 * half, 128), :] = lax.dot_general(
            flat[pl.ds(half, 8, stride=8), :], jnp.where(chunk == row, 1.0, 0.0).astype(F32),
            (((0,), (0,)), ((), ())), precision=HIGH, preferred_element_type=F32)
    cols = [cb[pl.ds(16 * m, 16), :] * (1.0 / SITES) for m in range(16)]
    line = lax.broadcasted_iota(jnp.int32, (16, 128), 0)
    inv = [jnp.where(line == m, 1.0, 0.0).astype(F32) for m in range(16)]
    for j in range(16):
        scale = 1.0 / jnp.sqrt(cols[j][j:j + 1])
        factor = jnp.where(line > j, cols[j] * scale, 0.0)
        for m in range(j + 1, 16):
            cols[m] = cols[m] - factor * (cols[m][j:j + 1] * scale)
        for m in range(j + 1):
            top = inv[m][j:j + 1] * scale
            inv[m] = jnp.where(line == j, top, inv[m] - factor * top)
    for m in range(16):
        cb[pl.ds(16 * m, 16), :] = inv[m]

    def entry(k, j):
        return jnp.broadcast_to(cb[pl.ds(16 * j + k, 1), :], (8, 128))

    def d_halo(n, h):
        part = pl.ds(12 * h, 12)
        return [
            remote(ee.at[n, pl.ds(4, 3), part], ee.at[n, pl.ds(0, 3), part],
                   dx_send.at[n, h, 0], dx_recv.at[n, h, 0], nxt),
            remote(ee.at[n, pl.ds(3, 3), part], ee.at[n, pl.ds(7, 3), part],
                   dx_send.at[n, h, 1], dx_recv.at[n, h, 1], prv),
            remote(ee.at[n, pl.ds(3, 4), part, pl.ds(5, 3)], hp.at[n, :, part, pl.ds(5, 3)],
                   dy_send.at[n, h, 0], dy_recv.at[n, h, 0], ynxt),
            remote(ee.at[n, pl.ds(3, 4), part, pl.ds(0, 3)], hn.at[n, :, part, pl.ds(0, 3)],
                   dy_send.at[n, h, 1], dy_recv.at[n, h, 1], yprv),
        ]

    d_copies = [None, None]
    for pair in range(8):
        same = [jnp.where(high_half, entry(pair + 8, j + 8), entry(pair, j)) for j in range(pair + 1)]
        cross = [jnp.where(high_half, entry(pair + 8, j), 0.0) for j in range(8)]

        def mix(x, total, pair=pair, same=same, cross=cross):
            for c in range(3):
                value = cross[0] * fps[x, c]
                for j in range(1, 8):
                    value = value + cross[j] * fps[x, j * 3 + c]
                for j in range(pair + 1):
                    value = value + same[j] * fp[x, j * 3 + c]
                ee[0, 3 + x, pair * 3 + c] = value
                total = total + value * value
            return total

        mom[0, pair] = lax.fori_loop(0, 4, mix, jnp.zeros((8, 128), F32))
        if pair & 3 == 3:
            d_copies[pair >> 2] = begin(d_halo(0, pair >> 2))

    def inner_pass(n, h, pi):
        def step(i, _):
            x = i
            base = 12 * h
            rho = (x + pi) & 1
            field = [[ee[n, 3 + x, base + v * 3 + c] for c in range(3)] for v in range(4)]
            acc = [[jnp.zeros((8, 128), F32)] * 3 for _ in range(4)]
            for d in range(8, 16):
                links = [ll[pi, x, d, e] for e in range(9)]
                hop = 3 if (d >> 1) & 1 else 1
                if d < 12:
                    idx = ix[ZZ + rho * 4 + (d - 8)]
                for v in range(4):
                    if d < 12:
                        moved = [lanes(f, idx) for f in field[v]]
                    else:
                        shift = 16 * hop if d & 1 else 128 - 16 * hop
                        moved = [pltpu.roll(f, shift, 1) for f in field[v]]
                    acc[v] = mul_add(acc[v], links, moved, d & 1)
            for v in range(4):
                for c in range(3):
                    h2[x, base + v * 3 + c] = acc[v][c]
            return 0

        lax.fori_loop(0, 4, step, 0)

    def outer_pass(n, h, pi, store):
        for v in range(4):
            mom[n + 1, 4 * h + v] = jnp.zeros((8, 128), F32)

        def step(i, _):
            x = i
            base = 12 * h
            acc = [[h2[x, base + v * 3 + c] for c in range(3)] for v in range(4)]
            for d in range(8):
                links = [ll[pi, x, d, e] for e in range(9)]
                hop = 3 if (d >> 1) & 1 else 1
                for v in range(4):
                    comps = [base + v * 3 + c for c in range(3)]
                    if d < 4:
                        moved = [ee[n, 3 + x - hop if d & 1 else 3 + x + hop, e] for e in comps]
                    elif d & 1:
                        moved = [pltpu.roll(jnp.where(row < 8 - hop, ee[n, 3 + x, e], hp[n, x, e]), hop, 0)
                                 for e in comps]
                    else:
                        moved = [pltpu.roll(jnp.where(row >= hop, ee[n, 3 + x, e], hn[n, x, e]), 8 - hop, 0)
                                 for e in comps]
                    acc[v] = mul_add(acc[v], links, moved, d & 1)
            for v in range(4):
                for c in range(3):
                    if store:
                        ee[n + 1, 3 + x, base + v * 3 + c] = acc[v][c]
                mom[n + 1, 4 * h + v] += (
                    acc[v][0] * acc[v][0] + acc[v][1] * acc[v][1] + acc[v][2] * acc[v][2])
            return 0

        lax.fori_loop(0, 4, step, 0)

    def flat_to_square(tile):
        total = jnp.zeros((16, 128), F32)
        for m in range(16):
            piece = jnp.broadcast_to(tile[m >> 3:(m >> 3) + 1], (16, 128))
            piece = pltpu.roll(piece, (128 - 16 * (m & 7)) & 127, 1) if m & 7 else piece
            total = jnp.where(line == m, piece, total)
        return total[:, :16]

    for n in range(3):
        pi = 1 - (n & 1)
        inner_pass(n, 0, pi)
        if n == 0:
            def keep_image(x, comp, acc):
                af[x, comp] = 6.0 * yy[3, 1 + x, comp] - acc

            for g in range(2):
                local_pass(3, g)
                end(halos[g])
                x_pass(3, g, lambda i: i, 4, keep_image)
            kone[0] = products(lambda x, e: yy[3, 1 + x, e], lambda x, e: af[x, e])
            k_partner = to_partner(kone, 1)
            k_partner.start()
        if n == 1:
            k_partner.wait()
            kslot[chip] = kone[0] + kone[1]
            k_chips = to_chips(kslot, 1)
            for c in k_chips:
                c.start()
        if n == 2:
            for c in k_chips:
                c.wait()
            square = flat_to_square(total_of(kslot))
            pick = jnp.where(lane == t * 16, 1.0, 0.0).astype(F32)
            weights = lax.dot_general(pick, cb[...], (((1,), (1,)), ((), ())),
                                      precision=HIGH, preferred_element_type=F32)
            weights = flat_to_square(jnp.where(row == 0, weights[:, :128], weights[:, 128:]))
            half = lax.dot_general(weights, square, (((0,), (0,)), ((), ())),
                                   precision=HIGH, preferred_element_type=F32)
            proj_ref[0] = lax.dot_general(half, weights, (((1,), (0,)), ((), ())),
                                          precision=HIGH, preferred_element_type=F32)
        for h in range(2):
            if h == 1:
                inner_pass(n, 1, pi)
            end(d_copies[h])
            outer_pass(n, h, pi, n < 2)
            if n < 2:
                d_copies[h] = begin(d_halo(n + 1, h))

    prod[...] = jnp.zeros((256, 128), F32)
    for m in range(4):
        for pair in range(8):
            prod[pl.ds(8 * m + pair, 1), :] = jnp.sum(mom[m, pair], axis=0, keepdims=True)
    select = jnp.where(((lane >> 3) & 1) == row, 1.0, 0.0).astype(F32)
    sone[0] = lax.dot_general(select, prod[pl.ds(0, 128), :], (((1,), (1,)), ((), ())),
                              precision=HIGH, preferred_element_type=F32)
    s_partner = to_partner(sone, 2)
    s_partner.start()
    s_partner.wait()
    sslot[chip] = sone[0] + sone[1]
    s_chips = to_chips(sslot, 2)
    for c in s_chips:
        c.start()
    for c in s_chips:
        c.wait()
    stm[t] = total_of(sslot)
    s_times = to_times(stm, 1)
    for c in s_times:
        c.start()
    for c in s_times:
        c.wait()
    n0 = total_of(stm)
    n1 = pltpu.roll(n0, 120, 1)
    n2 = pltpu.roll(n0, 112, 1)
    n3 = pltpu.roll(n0, 104, 1)
    ratio = n1 / n0
    alpha0 = 1.0 / (0.25 + ratio)
    rr = alpha0 * alpha0 * (n2 - ratio * n1)
    beta = rr / n0
    a = alpha0 * ratio + beta
    energy = 0.25 * rr * (1.0 + beta) + a * a * n1 - 2.0 * a * alpha0 * n2 + alpha0 * alpha0 * n3
    alpha1 = rr / energy
    first = alpha0 + alpha1 * a
    second = alpha1 * alpha0

    def spread(v, pair):
        low = jnp.broadcast_to(v[0:1, pair:pair + 1], (8, 128))
        high = jnp.broadcast_to(v[1:2, pair:pair + 1], (8, 128))
        return jnp.where(high_half, high, low)

    for pair in range(8):
        ca = spread(first, pair)
        cd = spread(second, pair)

        def finish_out(x, _, pair=pair, ca=ca, cd=cd):
            for c in range(3):
                value = ca * ee[0, 3 + x, pair * 3 + c] + cd * ee[2, 3 + x, pair * 3 + c]
                out_ref[pair, c, x] = lanes(value, ix[EX])
                out_ref[pair + 8, c, x] = lanes(value, ix[EX + 1])
            return 0

        lax.fori_loop(0, 4, finish_out, 0, unroll=True)


def rows_first(array, lead):
    return array.reshape(lead, 4, 8, 128).transpose(0, 2, 1, 3)


def body(start, smear_links, fat_links, naik_links):
    start = rows_first(start, 48).reshape(1536, 128)
    smear = rows_first(smear_links, 27).reshape(864, 128)
    fat = rows_first(fat_links, 36).reshape(4, 9, 8, 4, 128)
    naik = rows_first(naik_links, 36).reshape(4, 9, 8, 4, 128)
    vm = lambda *shape: pltpu.VMEM(shape, F32)
    dma = lambda *shape: pltpu.SemaphoreType.DMA(shape) if shape else pltpu.SemaphoreType.DMA
    anywhere = pl.BlockSpec(memory_space=pl.ANY)
    local = pl.BlockSpec(memory_space=pltpu.VMEM)
    projected, filled = pl.pallas_call(
        kernel,
        out_shape=(jax.ShapeDtypeStruct((1, 16, 16), F32),
                   jax.ShapeDtypeStruct((16, 3, 4, 8, 128), F32)),
        in_specs=[anywhere] * 4,
        out_specs=(local, local),
        scratch_shapes=[
            vm(1536, 128), vm(864, 128), vm(4, 6, 48, 8, 128), vm(5, 9, 8, 128), vm(4, 4, 9, 8, 128),
            vm(4, 48, 8, 128), vm(4, 48, 8, 128), vm(256, 128), vm(768, 128), vm(768, 128),
            vm(8, 2, 4, 6, 4, 128),
            vm(4, 2, 4, 9, 8, 128), vm(2, 4, 9, 8, 128), vm(2, 4, 9, 8, 128), vm(2, 4, 16, 9, 8, 128),
            vm(3, 10, 24, 8, 128), vm(3, 4, 24, 8, 128), vm(3, 4, 24, 8, 128), vm(4, 24, 8, 128),
            vm(4, 24, 8, 128), vm(4, 24, 8, 128), pltpu.VMEM((SLOTS, 8, 128), jnp.int32),
            vm(256, 128), vm(4, 8, 8, 128),
            vm(2, 8, 128), vm(8, 8, 128), vm(8, 8, 128),
            vm(2, 8, 128), vm(8, 8, 128),
            vm(2, 8, 128), vm(8, 8, 128), vm(8, 8, 128),
            dma(2), dma(4, 2, 2), dma(4, 2, 2), dma(), dma(), dma(2, 7), dma(2, 7), dma(2),
            dma(2, 2), dma(2, 2), dma(7), dma(7), dma(),
            dma(3, 2, 2), dma(3, 2, 2), dma(3, 2, 2), dma(3, 2, 2),
            dma(3), dma(3), dma(3, 7), dma(3, 7), dma(2, 7), dma(2, 7),
        ],
        compiler_params=pltpu.CompilerParams(
            collective_id=0, has_side_effects=True, vmem_limit_bytes=60 * 2**20),
        name="distill",
    )(start, smear, fat, naik)
    place = [lax.broadcasted_iota(jnp.int32, (4, 8, 128), d) for d in range(3)]
    even = ((place[0] + place[1] + (place[2] >> 4) + place[2]) & 1) == 0
    return projected * (1.0 / SITES), jnp.where(even, filled, 0.0)


def solution(mesh):
    in_specs = (
        P(None, None, "tm", "space", None),
        P(None, None, None, "tm", "space", None),
        P(None, None, None, "tm", "space", None),
        P(None, None, None, "tm", "space", None),
    )
    out_specs = (P("tm", None, None), P(None, None, "space", "tm", None))
    return jax.shard_map(body, mesh=mesh, in_specs=in_specs, out_specs=out_specs, check_vma=False)
```

```python
import functools
import jax
import jax.numpy as jnp
from jax import lax
from jax.sharding import PartitionSpec as P
import jax.experimental.pallas as pl
import jax.experimental.pallas.tpu as pltpu

MESH = pl.DeviceIdType.MESH
HIGH = lax.Precision.HIGHEST
F32 = jnp.float32
CENTER = 6.5
HALF_WIDTH = 5.5
ONE_HOP = 1.125
THREE_HOP = -1.0 / 24.0
SITES = 196608.0

ZP, ZM, PK, SKL, SUB, DSK, DSKS, CC, CT1, CT3, CZ1, CZ3, ZZ, EX, SLOTS = (
    0, 1, 2, 4, 5, 6, 7, 8, 10, 12, 14, 16, 18, 26, 28)


def lanes(v, idx):
    return jnp.take_along_axis(v, idx, axis=1, mode="promise_in_bounds")


def rows(v, idx):
    return jnp.take_along_axis(v, idx, axis=0, mode="promise_in_bounds")


def tile_iota():
    row = lax.broadcasted_iota(jnp.int32, (8, 128), 0)
    lane = lax.broadcasted_iota(jnp.int32, (8, 128), 1)
    return row, lane


def mul_add(acc, links, field, back):
    out = []
    for a in range(3):
        total = acc[a]
        for b in range(3):
            total = total + links[b * 3 + a if back else a * 3 + b] * field[b]
        out.append(total)
    return out


def fill_positions(ix, t):
    row, lane = tile_iota()
    chunk = lane >> 4
    low = lane & 15
    zc = lane & 7
    ix[ZP] = (chunk << 4) | ((low + 1) & 15)
    ix[ZM] = (chunk << 4) | ((low - 1) & 15)
    ysrc = (chunk - t) & 7
    for par in range(2):
        ix[PK + par] = (ysrc << 4) | (zc << 1) | ((t + par + ysrc) & 1)
    ix[SKL] = (((chunk - row) & 7) << 4) | low
    ix[SUB] = (chunk - row) & 7
    ix[DSK] = (((chunk + row) & 7) << 4) | low
    ix[DSKS] = (((chunk + row) & 7) << 4) | (low ^ 8)
    for rho in range(2):
        z = (zc << 1) | ((chunk + row + rho) & 1)
        ix[CC + rho] = (((chunk + row) & 7) << 4) | z
        ix[CT1 + rho] = (((chunk + row - 1) & 7) << 4) | z
        ix[CT3 + rho] = (((chunk + row - 3) & 7) << 4) | z
        ix[CZ1 + rho] = (((chunk + row) & 7) << 4) | ((z - 1) & 15)
        ix[CZ3 + rho] = (((chunk + row) & 7) << 4) | ((z - 3) & 15)
        for j, d in enumerate((1, -1, 3, -3)):
            ix[ZZ + rho * 4 + j] = (lane & 120) | (((z + d) & 15) >> 1)
    ix[EX] = (chunk << 4) | (low >> 1)
    ix[EX + 1] = (chunk << 4) | 8 | (low >> 1)


def kernel(start_ref, smear_ref, fat_ref, naik_ref, proj_ref, source_ref, second_ref, weight_ref,
           raw, sraw, yy, sx, syz, hh, af, prod, fs, fr, lraw, tl, tx, tyh, ll,
           ee, hn, hp, h2, fp, fps, ix, cb, mom, gone, gslot, gtm, sone, sslot, stm,
           in_sem, y_send, y_recv, sx_send, sx_recv, l_send, l_recv, l_own, lh_send, lh_recv,
           f_send, f_recv, f_own, dx_send, dx_recv, dy_send, dy_recv,
           c_send, c_recv, r_send, r_recv, t_send, t_recv, out_sem):
    t = lax.axis_index("tm")
    s = lax.axis_index("space")
    core = s & 1
    chip = s >> 1
    nxt = (t, (s + 1) & 15)
    prv = (t, (s + 15) & 15)
    ynxt = ((t + 1) & 7, s)
    yprv = ((t + 7) & 7, s)
    partner = (t, s + 1 - 2 * core)
    chips = [(t, (s + 2 * j) & 15) for j in range(1, 8)]
    times = [((t + d) & 7, s) for d in range(1, 8)]

    def remote(src, dst, send, recv, dev):
        return pltpu.make_async_remote_copy(src, dst, send, recv, device_id=dev, device_id_type=MESH)

    load_start = pltpu.make_async_copy(start_ref, raw, in_sem.at[0])
    load_smear = pltpu.make_async_copy(smear_ref, sraw, in_sem.at[1])
    load_start.start()
    load_smear.start()
    own_links = [
        pltpu.make_async_copy(ref.at[:, pl.ds(0, 6), t], lraw.at[t, i], l_own.at[i])
        for i, ref in enumerate((fat_ref, naik_ref))
    ]
    for c in own_links:
        c.start()

    barrier = pltpu.get_barrier_semaphore()
    friends = [nxt, prv] + chips + times
    for dev in friends:
        pl.semaphore_signal(barrier, inc=1, device_id=dev, device_id_type=MESH)

    fill_positions(ix, t)
    row, lane = tile_iota()
    high_half = (lane & 8) != 0

    load_start.wait()

    def place_start(i, _):
        for x in range(4):
            yy[0, 1 + x, i] = raw[pl.ds(i * 32 + x, 8, stride=4), :]
        return 0

    lax.fori_loop(0, 48, place_start, 0, unroll=4)
    pl.semaphore_wait(barrier, len(friends))

    def halo(n, h):
        part = pl.ds(24 * h, 24)
        return [
            remote(yy.at[n, 4, part], yy.at[n, 0, part], y_send.at[n, h, 0], y_recv.at[n, h, 0], nxt),
            remote(yy.at[n, 1, part], yy.at[n, 5, part], y_send.at[n, h, 1], y_recv.at[n, h, 1], prv),
        ]

    def begin(copies):
        for c in copies:
            c.start()
        return copies

    def end(copies):
        for c in copies:
            c.wait()

    halos = [begin(halo(0, h)) for h in range(2)]

    load_smear.wait()

    def ahead_y(v):
        r = pltpu.roll(v, 112, 1)
        return jnp.where(lane < 112, r, pltpu.roll(r, 7, 0))

    def behind_y(v):
        r = pltpu.roll(v, 16, 1)
        return jnp.where(lane >= 16, r, pltpu.roll(r, 1, 0))

    zp_i = ix[ZP]
    zm_i = ix[ZM]

    def place_smear(i, _):
        for x in range(4):
            sx[1 + x, i] = sraw[pl.ds(i * 32 + x, 8, stride=4), :]
            ly = sraw[pl.ds((9 + i) * 32 + x, 8, stride=4), :]
            lz = sraw[pl.ds((18 + i) * 32 + x, 8, stride=4), :]
            syz[x, 0, i] = ly
            syz[x, 1, i] = behind_y(ly)
            syz[x, 2, i] = lz
            syz[x, 3, i] = lanes(lz, zm_i)
        return 0

    lax.fori_loop(0, 9, place_smear, 0)
    sx_copy = remote(sx.at[4], sx.at[0], sx_send, sx_recv, nxt)
    sx_copy.start()

    link_copies = []
    for d in range(1, 8):
        dest = (t + d) & 7
        for i, ref in enumerate((fat_ref, naik_ref)):
            c = remote(ref.at[:, pl.ds(0, 6), dest], lraw.at[t, i],
                       l_send.at[i, d - 1], l_recv.at[i, d - 1], (dest, s))
            c.start()
            link_copies.append(c)

    def local_pass(n, h):
        def step(i, _):
            x = i >> 1
            base = 24 * h + (i & 1) * 12
            field = [[yy[n, 1 + x, base + v * 3 + c] for c in range(3)] for v in range(4)]
            acc = [[jnp.zeros((8, 128), F32)] * 3 for _ in range(4)]
            for d in range(4):
                links = [syz[x, d, e] for e in range(9)]
                for v in range(4):
                    if d == 0:
                        moved = [ahead_y(f) for f in field[v]]
                    elif d == 1:
                        moved = [behind_y(f) for f in field[v]]
                    else:
                        moved = [lanes(f, zp_i if d == 2 else zm_i) for f in field[v]]
                    acc[v] = mul_add(acc[v], links, moved, d & 1)
            for v in range(4):
                for c in range(3):
                    hh[x, base + v * 3 + c] = acc[v][c]
            return 0

        lax.fori_loop(0, 8, step, 0)

    def x_pass(n, h, plane_of, count, finish):
        def step(i, _):
            x = plane_of(i >> 1)
            base = 24 * h + (i & 1) * 12
            for back in (False, True):
                links = [sx[x if back else 1 + x, e] for e in range(9)]
                for v in range(4):
                    field = [yy[n, x if back else 2 + x, base + v * 3 + c] for c in range(3)]
                    acc = [hh[x, base + v * 3 + c] for c in range(3)] if not back else keep[v]
                    acc = mul_add(acc, links, field, back)
                    if not back:
                        if v == 0:
                            keep = []
                        keep.append(acc)
                    else:
                        for c in range(3):
                            finish(x, base + v * 3 + c, acc[c])
            return 0

        lax.fori_loop(0, 2 * count, step, 0)

    lflat = lraw.reshape(8 * 192, 128)

    def place_links(i, _):
        kind = i >> 2
        mu = i & 3
        for x in range(4):
            tiles = []
            for e in range(6):
                v = lanes(lflat[pl.ds(i * 24 + e * 4 + x, 8, stride=192), :], ix[SKL])
                tiles.append(rows(v, ix[SUB]))
            for a in range(3):
                b, c = (a + 1) % 3, (a + 2) % 3
                tiles.append(tiles[b] * tiles[3 + c] - tiles[c] * tiles[3 + b])
            for e in range(9):
                tl[x, kind, mu, e] = tiles[e]
        return 0

    for n in range(3):
        for h in range(2):
            local_pass(n, h)
            if n == 0 and h == 0:
                sx_copy.wait()
            if n == 2 and h == 0:
                for c in own_links + link_copies:
                    c.wait()
                lax.fori_loop(0, 8, place_links, 0)
                link_halos = [
                    remote(tl.at[3, 0, 0], tx.at[0, 3], lh_send.at[0, 0], lh_recv.at[0, 0], nxt),
                    remote(tl.at[pl.ds(1, 3), 1, 0], tx.at[1, pl.ds(1, 3)], lh_send.at[0, 1], lh_recv.at[0, 1], nxt),
                    remote(tl.at[:, 0, 1, :, pl.ds(7, 1)], tyh.at[0, :, :, pl.ds(7, 1)],
                           lh_send.at[1, 0], lh_recv.at[1, 0], ynxt),
                    remote(tl.at[:, 1, 1, :, pl.ds(5, 3)], tyh.at[1, :, :, pl.ds(5, 3)],
                           lh_send.at[1, 1], lh_recv.at[1, 1], ynxt),
                ]
            end(halos[h])

            def finish(x, comp, acc, n=n):
                if n == 0:
                    value = (-0.5 / HALF_WIDTH) * yy[0, 1 + x, comp] - (1.0 / HALF_WIDTH) * acc
                else:
                    value = ((-1.0 / HALF_WIDTH) * yy[n, 1 + x, comp] - (2.0 / HALF_WIDTH) * acc
                             - yy[n - 1, 1 + x, comp])
                yy[n + 1, 1 + x, comp] = value

            x_pass(n, h, lambda i: 3 * i, 2, finish)
            if n < 2:
                halos[h] = begin(halo(n + 1, h))
            if n == 2 and h == 0:
                begin(link_halos)
            x_pass(n, h, lambda i: 1 + i, 2, finish)

    def products(left, right):
        def step(k, _):
            mine = [left(x, k * 3 + c) for x in range(4) for c in range(3)]
            for d in range(9):
                j = (k + d) & 15
                total = None
                for x in range(4):
                    for c in range(3):
                        term = mine[x * 3 + c] * right(x, j * 3 + c)
                        total = term if total is None else total + term
                total = jnp.sum(total, axis=0, keepdims=True)
                prod[pl.ds(j * 16 + k, 1), :] = total
                prod[pl.ds(k * 16 + j, 1), :] = total
            return 0

        lax.fori_loop(0, 16, step, 0)
        sums = lax.dot_general(jnp.ones((8, 128), F32), prod[...], (((1,), (1,)), ((), ())),
                               precision=HIGH, preferred_element_type=F32)
        return jnp.where(row == 0, sums[:, :128], sums[:, 128:])

    def to_partner(buf, which):
        return remote(buf.at[0], buf.at[1], c_send.at[which], c_recv.at[which], partner)

    def to_chips(buf, which):
        return [remote(buf.at[chip], buf.at[chip], r_send.at[which, j], r_recv.at[which, j], chips[j])
                for j in range(7)]

    def to_times(buf, which):
        return [remote(buf.at[t], buf.at[t], t_send.at[which, j], t_recv.at[which, j], times[j])
                for j in range(7)]

    def total_of(buf):
        total = buf[0]
        for j in range(1, 8):
            total = total + buf[j]
        return total

    gone[0] = products(lambda x, e: yy[3, 1 + x, e], lambda x, e: yy[3, 1 + x, e])
    g_partner = to_partner(gone, 0)
    g_partner.start()
    def pack(i, _):
        x = i >> 3
        pair = i & 7
        idx = ix[PK + (x & 1)]
        for c in range(3):
            one = lanes(yy[3, 1 + x, pair * 3 + c], idx)
            two = lanes(yy[3, 1 + x, pair * 3 + 24 + c], idx)
            fs[pl.ds(x * 24 + pair * 3 + c, 8, stride=96), :] = jnp.where(high_half, two, one)
        return 0

    lax.fori_loop(0, 32, pack, 0)

    def part(ref, which):
        return ref.at[pl.ds(pl.multiple_of(which * 96, 96), 96)]

    f_copies = [
        remote(part(fs, (t + d) & 7), part(fr, t), f_send.at[d - 1], f_recv.at[d - 1], times[d - 1])
        for d in range(1, 8)
    ]
    f_local = pltpu.make_async_copy(part(fs, t), part(fr, t), f_own)

    g_partner.wait()
    gslot[chip] = gone[0] + gone[1]
    g_chips = to_chips(gslot, 0)
    for c in g_chips:
        c.start()
    for c in f_copies + [f_local]:
        c.start()

    halos = [begin(halo(3, h)) for h in range(2)]
    chunk = lane >> 4

    def fill_links(i, _):
        x = i & 3
        e = i >> 2
        xsign = (1 - 2 * (x & 1)).astype(F32)
        ysign = (1 - 2 * (row & 1)).astype(F32)
        tsign = (1 - 2 * (chunk & 1)).astype(F32)
        for kind, hop, weight in ((0, 1, 0.5 * ONE_HOP), (1, 3, 0.5 * THREE_HOP)):
            px = x - hop
            own = [tl[x, kind, mu, e] for mu in range(4)]
            before_x = jnp.where(px >= 0, tl[jnp.maximum(px, 0), kind, 0, e],
                                 tx[kind, jnp.minimum(px + 4, 3), e])
            before_y = pltpu.roll(jnp.where(row < 8 - hop, own[1], tyh[kind, x, e]), hop, 0)
            for pi in range(2):
                rho = (x + pi) & 1
                cc = ix[CC + rho]
                ct = ix[(CT3 if kind else CT1) + rho]
                cz = ix[(CZ3 if kind else CZ1) + rho]
                pis = -1.0 if pi else 1.0
                scale = [
                    jnp.full((8, 128), weight, F32),
                    jnp.full((8, 128), weight, F32) * xsign,
                    weight * xsign * ysign,
                ]
                fwd = [lanes(own[mu], cc) for mu in range(4)]
                bwd = [lanes(before_x, cc), lanes(before_y, ct), lanes(own[2], cz), lanes(own[3], ct)]
                for mu in range(4):
                    if mu < 3:
                        up, down = scale[mu], -scale[mu]
                    else:
                        up = jnp.where(chunk < 8 - hop, (pis * weight) * tsign, 0.0)
                        down = jnp.where(chunk >= hop, (-pis * weight) * tsign, 0.0)
                    ll[pi, x, (mu * 2 + kind) * 2, e] = up * fwd[mu]
                    ll[pi, x, (mu * 2 + kind) * 2 + 1, e] = down * bwd[mu]
        return 0

    end(link_halos)
    lax.fori_loop(0, 12, fill_links, 0)

    for c in g_chips:
        c.wait()
    gtm[t] = total_of(gslot)
    g_times = to_times(gtm, 0)
    for c in g_times:
        c.start()
    lax.fori_loop(12, 36, fill_links, 0)

    for c in f_copies:
        c.wait()
    f_local.wait()

    def unpack(i, _):
        x = i >> 1
        for c in range(12):
            e = (i & 1) * 12 + c
            v = rows(fr[pl.ds(x * 24 + e, 8, stride=96), :], ix[SUB])
            fp[x, e] = lanes(v, ix[DSK])
            fps[x, e] = lanes(v, ix[DSKS])
        return 0

    lax.fori_loop(0, 8, unpack, 0)

    for c in g_times:
        c.wait()

    flat = gtm.reshape(64, 128)
    for half in range(2):
        cb[pl.ds(128 * half, 128), :] = lax.dot_general(
            flat[pl.ds(half, 8, stride=8), :], jnp.where(chunk == row, 1.0, 0.0).astype(F32),
            (((0,), (0,)), ((), ())), precision=HIGH, preferred_element_type=F32)
    cols = [cb[pl.ds(16 * m, 16), :] * (1.0 / SITES) for m in range(16)]
    line = lax.broadcasted_iota(jnp.int32, (16, 128), 0)
    inv = [jnp.where(line == m, 1.0, 0.0).astype(F32) for m in range(16)]
    for j in range(16):
        scale = 1.0 / jnp.sqrt(cols[j][j:j + 1])
        factor = jnp.where(line > j, cols[j] * scale, 0.0)
        for m in range(j + 1, 16):
            cols[m] = cols[m] - factor * (cols[m][j:j + 1] * scale)
        for m in range(j + 1):
            top = inv[m][j:j + 1] * scale
            inv[m] = jnp.where(line == j, top, inv[m] - factor * top)
    for m in range(16):
        cb[pl.ds(16 * m, 16), :] = inv[m]

    def entry(k, j):
        return jnp.broadcast_to(cb[pl.ds(16 * j + k, 1), :], (8, 128))

    def d_halo(n, h):
        part = pl.ds(12 * h, 12)
        return [
            remote(ee.at[n, pl.ds(4, 3), part], ee.at[n, pl.ds(0, 3), part],
                   dx_send.at[n, h, 0], dx_recv.at[n, h, 0], nxt),
            remote(ee.at[n, pl.ds(3, 3), part], ee.at[n, pl.ds(7, 3), part],
                   dx_send.at[n, h, 1], dx_recv.at[n, h, 1], prv),
            remote(ee.at[n, pl.ds(3, 4), part, pl.ds(5, 3)], hp.at[n, :, part, pl.ds(5, 3)],
                   dy_send.at[n, h, 0], dy_recv.at[n, h, 0], ynxt),
            remote(ee.at[n, pl.ds(3, 4), part, pl.ds(0, 3)], hn.at[n, :, part, pl.ds(0, 3)],
                   dy_send.at[n, h, 1], dy_recv.at[n, h, 1], yprv),
        ]

    d_copies = [None, None]
    for pair in range(8):
        same = [jnp.where(high_half, entry(pair + 8, j + 8), entry(pair, j)) for j in range(pair + 1)]
        cross = [jnp.where(high_half, entry(pair + 8, j), 0.0) for j in range(8)]

        def mix(x, total, pair=pair, same=same, cross=cross):
            for c in range(3):
                value = cross[0] * fps[x, c]
                for j in range(1, 8):
                    value = value + cross[j] * fps[x, j * 3 + c]
                for j in range(pair + 1):
                    value = value + same[j] * fp[x, j * 3 + c]
                ee[0, 3 + x, pair * 3 + c] = value
                total = total + value * value
            return total

        mom[0, pair] = lax.fori_loop(0, 4, mix, jnp.zeros((8, 128), F32))
        if pair & 3 == 3:
            d_copies[pair >> 2] = begin(d_halo(0, pair >> 2))

    def inner_pass(n, h, pi):
        def step(i, _):
            x = i
            base = 12 * h
            rho = (x + pi) & 1
            field = [[ee[n, 3 + x, base + v * 3 + c] for c in range(3)] for v in range(4)]
            acc = [[jnp.zeros((8, 128), F32)] * 3 for _ in range(4)]
            for d in range(8, 16):
                links = [ll[pi, x, d, e] for e in range(9)]
                hop = 3 if (d >> 1) & 1 else 1
                if d < 12:
                    idx = ix[ZZ + rho * 4 + (d - 8)]
                for v in range(4):
                    if d < 12:
                        moved = [lanes(f, idx) for f in field[v]]
                    else:
                        shift = 16 * hop if d & 1 else 128 - 16 * hop
                        moved = [pltpu.roll(f, shift, 1) for f in field[v]]
                    acc[v] = mul_add(acc[v], links, moved, d & 1)
            for v in range(4):
                for c in range(3):
                    h2[x, base + v * 3 + c] = acc[v][c]
            return 0

        lax.fori_loop(0, 4, step, 0)

    def outer_pass(n, h, pi, store):
        for v in range(4):
            mom[n + 1, 4 * h + v] = jnp.zeros((8, 128), F32)

        def step(i, _):
            x = i
            base = 12 * h
            acc = [[h2[x, base + v * 3 + c] for c in range(3)] for v in range(4)]
            for d in range(8):
                links = [ll[pi, x, d, e] for e in range(9)]
                hop = 3 if (d >> 1) & 1 else 1
                for v in range(4):
                    comps = [base + v * 3 + c for c in range(3)]
                    if d < 4:
                        moved = [ee[n, 3 + x - hop if d & 1 else 3 + x + hop, e] for e in comps]
                    elif d & 1:
                        moved = [pltpu.roll(jnp.where(row < 8 - hop, ee[n, 3 + x, e], hp[n, x, e]), hop, 0)
                                 for e in comps]
                    else:
                        moved = [pltpu.roll(jnp.where(row >= hop, ee[n, 3 + x, e], hn[n, x, e]), 8 - hop, 0)
                                 for e in comps]
                    acc[v] = mul_add(acc[v], links, moved, d & 1)
            for v in range(4):
                for c in range(3):
                    if store:
                        ee[n + 1, 3 + x, base + v * 3 + c] = acc[v][c]
                mom[n + 1, 4 * h + v] += (
                    acc[v][0] * acc[v][0] + acc[v][1] * acc[v][1] + acc[v][2] * acc[v][2])
            return 0

        lax.fori_loop(0, 4, step, 0)

    def flat_to_square(tile):
        total = jnp.zeros((16, 128), F32)
        for m in range(16):
            piece = jnp.broadcast_to(tile[m >> 3:(m >> 3) + 1], (16, 128))
            piece = pltpu.roll(piece, (128 - 16 * (m & 7)) & 127, 1) if m & 7 else piece
            total = jnp.where(line == m, piece, total)
        return total[:, :16]

    for n in range(3):
        pi = 1 - (n & 1)
        inner_pass(n, 0, pi)
        if n == 0:
            def keep_image(x, comp, acc):
                af[x, comp] = 6.0 * yy[3, 1 + x, comp] - acc

            for g in range(2):
                local_pass(3, g)
                end(halos[g])
                x_pass(3, g, lambda i: i, 4, keep_image)
            sone[0, 1] = products(lambda x, e: yy[3, 1 + x, e], lambda x, e: af[x, e])
        for h in range(2):
            if h == 1:
                inner_pass(n, 1, pi)
            end(d_copies[h])
            outer_pass(n, h, pi, n < 2)
            if n < 2:
                d_copies[h] = begin(d_halo(n + 1, h))

    saved = [pltpu.make_async_copy(ee.at[2 * i, pl.ds(3, 4)], ref, out_sem.at[i])
             for i, ref in enumerate((source_ref, second_ref))]
    for c in saved:
        c.start()

    prod[...] = jnp.zeros((256, 128), F32)
    for m in range(4):
        for pair in range(8):
            prod[pl.ds(8 * m + pair, 1), :] = jnp.sum(mom[m, pair], axis=0, keepdims=True)
    select = jnp.where(((lane >> 3) & 1) == row, 1.0, 0.0).astype(F32)
    sone[0, 0] = lax.dot_general(select, prod[pl.ds(0, 128), :], (((1,), (1,)), ((), ())),
                              precision=HIGH, preferred_element_type=F32)
    s_partner = to_partner(sone, 1)
    s_partner.start()
    s_partner.wait()
    sslot[chip] = sone[0] + sone[1]
    s_chips = to_chips(sslot, 1)
    for c in s_chips:
        c.start()
    for c in s_chips:
        c.wait()
    both = total_of(sslot)
    stm[t] = both[0]
    s_times = to_times(stm, 1)
    for c in s_times:
        c.start()

    square = flat_to_square(both[1])
    pick = jnp.where(lane == t * 16, 1.0, 0.0).astype(F32)
    weights = lax.dot_general(pick, cb[...], (((1,), (1,)), ((), ())),
                              precision=HIGH, preferred_element_type=F32)
    weights = flat_to_square(jnp.where(row == 0, weights[:, :128], weights[:, 128:]))
    half = lax.dot_general(weights, square, (((0,), (0,)), ((), ())),
                           precision=HIGH, preferred_element_type=F32)
    proj_ref[0] = lax.dot_general(half, weights, (((1,), (0,)), ((), ())),
                                  precision=HIGH, preferred_element_type=F32) * (1.0 / SITES)
    for c in s_times:
        c.wait()
    n0 = total_of(stm)
    n1 = pltpu.roll(n0, 120, 1)
    n2 = pltpu.roll(n0, 112, 1)
    n3 = pltpu.roll(n0, 104, 1)
    ratio = n1 / n0
    alpha0 = 1.0 / (0.25 + ratio)
    rr = alpha0 * alpha0 * (n2 - ratio * n1)
    beta = rr / n0
    a = alpha0 * ratio + beta
    energy = 0.25 * rr * (1.0 + beta) + a * a * n1 - 2.0 * a * alpha0 * n2 + alpha0 * alpha0 * n3
    alpha1 = rr / energy
    weight_ref[...] = jnp.where(row < 2, alpha1 * alpha0, pltpu.roll(alpha0 + alpha1 * a, 2, 0))
    for c in saved:
        c.wait()


def assemble(proj_ref, source_ref, second_ref, weight_ref, done_ref, out_ref,
             small, weights, pp, ww, full, in_sem, out_sem):
    loads = [pltpu.make_async_copy(weight_ref, weights, in_sem.at[0]),
             pltpu.make_async_copy(proj_ref, small, in_sem.at[1])]
    parts = [pl.ds(6 * i, 6) for i in range(4)]
    fields = [
        [pltpu.make_async_copy(ref.at[:, part], buf.at[:, part], in_sem.at[2 + 2 * i + j])
         for j, (ref, buf) in enumerate(((source_ref, pp), (second_ref, ww)))]
        for i, part in enumerate(parts)
    ]
    for c in loads + sum(fields, []):
        c.start()
    row, lane = tile_iota()
    high_half = (lane & 8) != 0
    spots = [(lane & 112) | 8 * h | ((lane & 15) >> 1) for h in range(2)]
    even = [((x + row + (lane >> 4) + lane) & 1) == 0 for x in range(2)]
    for c in loads:
        c.wait()
    done = pltpu.make_async_copy(small, done_ref, out_sem.at[0])
    done.start()
    stores = [done]

    def spread(first, pair):
        low = jnp.broadcast_to(weights[first:first + 1, pair:pair + 1], (8, 128))
        high = jnp.broadcast_to(weights[first + 1:first + 2, pair:pair + 1], (8, 128))
        return jnp.where(high_half, high, low)

    for i in range(4):
        for c in fields[i]:
            c.wait()
        for pair in (2 * i, 2 * i + 1):
            ca = spread(2, pair)
            cd = spread(0, pair)
            for x in range(4):
                for c in range(3):
                    value = ca * pp[x, pair * 3 + c] + cd * ww[x, pair * 3 + c]
                    for h in range(2):
                        full[pair + 8 * h, c, x] = jnp.where(even[x & 1], lanes(value, spots[h]), 0.0)
        for h in range(2):
            where = pl.ds(8 * h + 2 * i, 2)
            copy = pltpu.make_async_copy(full.at[where], out_ref.at[where], out_sem.at[1 + 2 * i + h])
            copy.start()
            stores.append(copy)
    for c in stores:
        c.wait()


def rows_first(array, lead):
    return array.reshape(lead, 4, 8, 128).transpose(0, 2, 1, 3)


def body(start, smear_links, fat_links, naik_links):
    start = rows_first(start, 48).reshape(1536, 128)
    smear = rows_first(smear_links, 27).reshape(864, 128)
    fat = rows_first(fat_links, 36).reshape(4, 9, 8, 4, 128)
    naik = rows_first(naik_links, 36).reshape(4, 9, 8, 4, 128)
    vm = lambda *shape: pltpu.VMEM(shape, F32)
    dma = lambda *shape: pltpu.SemaphoreType.DMA(shape) if shape else pltpu.SemaphoreType.DMA
    anywhere = pl.BlockSpec(memory_space=pl.ANY)
    local = pl.BlockSpec(memory_space=pltpu.VMEM)
    packed = jax.ShapeDtypeStruct((4, 24, 8, 128), F32)
    parts = pl.pallas_call(
        kernel,
        out_shape=(jax.ShapeDtypeStruct((1, 16, 16), F32), packed, packed,
                   jax.ShapeDtypeStruct((8, 128), F32)),
        in_specs=[anywhere] * 4,
        out_specs=(local, anywhere, anywhere, local),
        scratch_shapes=[
            vm(1536, 128), vm(864, 128), vm(4, 6, 48, 8, 128), vm(5, 9, 8, 128), vm(4, 4, 9, 8, 128),
            vm(4, 48, 8, 128), vm(4, 48, 8, 128), vm(256, 128), vm(768, 128), vm(768, 128),
            vm(8, 2, 4, 6, 4, 128),
            vm(4, 2, 4, 9, 8, 128), vm(2, 4, 9, 8, 128), vm(2, 4, 9, 8, 128), vm(2, 4, 16, 9, 8, 128),
            vm(3, 10, 24, 8, 128), vm(3, 4, 24, 8, 128), vm(3, 4, 24, 8, 128), vm(4, 24, 8, 128),
            vm(4, 24, 8, 128), vm(4, 24, 8, 128), pltpu.VMEM((SLOTS, 8, 128), jnp.int32),
            vm(256, 128), vm(4, 8, 8, 128),
            vm(2, 8, 128), vm(8, 8, 128), vm(8, 8, 128),
            vm(2, 2, 8, 128), vm(8, 2, 8, 128), vm(8, 8, 128),
            dma(2), dma(4, 2, 2), dma(4, 2, 2), dma(), dma(), dma(2, 7), dma(2, 7), dma(2),
            dma(2, 2), dma(2, 2), dma(7), dma(7), dma(),
            dma(3, 2, 2), dma(3, 2, 2), dma(3, 2, 2), dma(3, 2, 2),
            dma(2), dma(2), dma(2, 7), dma(2, 7), dma(2, 7), dma(2, 7), dma(2),
        ],
        compiler_params=pltpu.CompilerParams(
            collective_id=0, has_side_effects=True, vmem_limit_bytes=60 * 2**20),
        name="distill",
    )(start, smear, fat, naik)
    return pl.pallas_call(
        assemble,
        out_shape=(jax.ShapeDtypeStruct((1, 16, 16), F32),
                   jax.ShapeDtypeStruct((16, 3, 4, 8, 128), F32)),
        in_specs=[anywhere] * 4,
        out_specs=(anywhere, anywhere),
        scratch_shapes=[vm(1, 16, 16), vm(8, 128), vm(4, 24, 8, 128), vm(4, 24, 8, 128),
                        vm(16, 3, 4, 8, 128), dma(10), dma(9)],
        compiler_params=pltpu.CompilerParams(vmem_limit_bytes=60 * 2**20),
        name="assemble",
    )(*parts)


def solution(mesh):
    in_specs = (
        P(None, None, "tm", "space", None),
        P(None, None, None, "tm", "space", None),
        P(None, None, None, "tm", "space", None),
        P(None, None, None, "tm", "space", None),
    )
    out_specs = (P("tm", None, None), P(None, None, "space", "tm", None))
    return jax.shard_map(body, mesh=mesh, in_specs=in_specs, out_specs=out_specs, check_vma=False)
```

```python
import functools
import jax
import jax.numpy as jnp
from jax import lax
from jax.sharding import PartitionSpec as P
import jax.experimental.pallas as pl
import jax.experimental.pallas.tpu as pltpu

MESH = pl.DeviceIdType.MESH
HIGH = lax.Precision.HIGHEST
F32 = jnp.float32
CENTER = 6.5
HALF_WIDTH = 5.5
ONE_HOP = 1.125
THREE_HOP = -1.0 / 24.0
SITES = 196608.0

ZP, ZM, PK, SKL, SUB, DSK, DSKS, CC, CT1, CT3, CZ1, CZ3, ZZ, EX, SLOTS = (
    0, 1, 2, 4, 5, 6, 7, 8, 10, 12, 14, 16, 18, 26, 28)


def lanes(v, idx):
    return jnp.take_along_axis(v, idx, axis=1, mode="promise_in_bounds")


def rows(v, idx):
    return jnp.take_along_axis(v, idx, axis=0, mode="promise_in_bounds")


def tile_iota():
    row = lax.broadcasted_iota(jnp.int32, (8, 128), 0)
    lane = lax.broadcasted_iota(jnp.int32, (8, 128), 1)
    return row, lane


def mul_add(acc, links, field, back):
    out = []
    for a in range(3):
        total = acc[a]
        for b in range(3):
            total = total + links[b * 3 + a if back else a * 3 + b] * field[b]
        out.append(total)
    return out


def fill_positions(ix, t):
    row, lane = tile_iota()
    chunk = lane >> 4
    low = lane & 15
    zc = lane & 7
    ix[ZP] = (chunk << 4) | ((low + 1) & 15)
    ix[ZM] = (chunk << 4) | ((low - 1) & 15)
    ysrc = (chunk - t) & 7
    for par in range(2):
        ix[PK + par] = (ysrc << 4) | (zc << 1) | ((t + par + ysrc) & 1)
    ix[SKL] = (((chunk - row) & 7) << 4) | low
    ix[SUB] = (chunk - row) & 7
    ix[DSK] = (((chunk + row) & 7) << 4) | low
    ix[DSKS] = (((chunk + row) & 7) << 4) | (low ^ 8)
    for rho in range(2):
        z = (zc << 1) | ((chunk + row + rho) & 1)
        ix[CC + rho] = (((chunk + row) & 7) << 4) | z
        ix[CT1 + rho] = (((chunk + row - 1) & 7) << 4) | z
        ix[CT3 + rho] = (((chunk + row - 3) & 7) << 4) | z
        ix[CZ1 + rho] = (((chunk + row) & 7) << 4) | ((z - 1) & 15)
        ix[CZ3 + rho] = (((chunk + row) & 7) << 4) | ((z - 3) & 15)
        for j, d in enumerate((1, -1, 3, -3)):
            ix[ZZ + rho * 4 + j] = (lane & 120) | (((z + d) & 15) >> 1)
    ix[EX] = (chunk << 4) | (low >> 1)
    ix[EX + 1] = (chunk << 4) | 8 | (low >> 1)


def kernel(start_ref, smear_ref, fat_ref, naik_ref, proj_ref, source_ref, second_ref, weight_ref,
           raw, sraw, yy, sx, syz, hh, af, prod, fs, fr, lraw, tl, tx, tyh, ll,
           ee, hn, hp, h2, fp, fps, ix, cb, mom, gone, gslot, gtm, sone, sslot, stm,
           in_sem, y_send, y_recv, sx_send, sx_recv, l_send, l_recv, l_own, lh_send, lh_recv,
           f_send, f_recv, f_own, dx_send, dx_recv, dy_send, dy_recv,
           c_send, c_recv, r_send, r_recv, t_send, t_recv, out_sem):
    t = lax.axis_index("tm")
    s = lax.axis_index("space")
    core = s & 1
    chip = s >> 1
    nxt = (t, (s + 1) & 15)
    prv = (t, (s + 15) & 15)
    ynxt = ((t + 1) & 7, s)
    yprv = ((t + 7) & 7, s)
    partner = (t, s + 1 - 2 * core)
    chips = [(t, (s + 2 * j) & 15) for j in range(1, 8)]
    times = [((t + d) & 7, s) for d in range(1, 8)]

    def remote(src, dst, send, recv, dev):
        return pltpu.make_async_remote_copy(src, dst, send, recv, device_id=dev, device_id_type=MESH)

    load_start = pltpu.make_async_copy(start_ref, raw, in_sem.at[0])
    load_smear = pltpu.make_async_copy(smear_ref, sraw, in_sem.at[1])
    load_start.start()
    load_smear.start()
    own_links = [
        pltpu.make_async_copy(ref.at[:, pl.ds(0, 6), t], lraw.at[t, i], l_own.at[i])
        for i, ref in enumerate((fat_ref, naik_ref))
    ]
    for c in own_links:
        c.start()

    barrier = pltpu.get_barrier_semaphore()
    friends = [nxt, prv] + chips + times
    for dev in friends:
        pl.semaphore_signal(barrier, inc=1, device_id=dev, device_id_type=MESH)

    fill_positions(ix, t)
    row, lane = tile_iota()
    high_half = (lane & 8) != 0

    load_start.wait()

    def place_start(i, _):
        for x in range(4):
            yy[0, 1 + x, i] = raw[pl.ds(i * 32 + x, 8, stride=4), :]
        return 0

    lax.fori_loop(0, 48, place_start, 0, unroll=4)
    pl.semaphore_wait(barrier, len(friends))

    def halo(n, h):
        part = pl.ds(24 * h, 24)
        return [
            remote(yy.at[n, 4, part], yy.at[n, 0, part], y_send.at[n, h, 0], y_recv.at[n, h, 0], nxt),
            remote(yy.at[n, 1, part], yy.at[n, 5, part], y_send.at[n, h, 1], y_recv.at[n, h, 1], prv),
        ]

    def begin(copies):
        for c in copies:
            c.start()
        return copies

    def end(copies):
        for c in copies:
            c.wait()

    halos = [begin(halo(0, h)) for h in range(2)]

    load_smear.wait()

    def ahead_y(v):
        r = pltpu.roll(v, 112, 1)
        return jnp.where(lane < 112, r, pltpu.roll(r, 7, 0))

    def behind_y(v):
        r = pltpu.roll(v, 16, 1)
        return jnp.where(lane >= 16, r, pltpu.roll(r, 1, 0))

    zp_i = ix[ZP]
    zm_i = ix[ZM]

    def place_smear(i, _):
        for x in range(4):
            sx[1 + x, i] = sraw[pl.ds(i * 32 + x, 8, stride=4), :]
            ly = sraw[pl.ds((9 + i) * 32 + x, 8, stride=4), :]
            lz = sraw[pl.ds((18 + i) * 32 + x, 8, stride=4), :]
            syz[x, 0, i] = ly
            syz[x, 1, i] = behind_y(ly)
            syz[x, 2, i] = lz
            syz[x, 3, i] = lanes(lz, zm_i)
        return 0

    lax.fori_loop(0, 9, place_smear, 0)
    sx_copy = remote(sx.at[4], sx.at[0], sx_send, sx_recv, nxt)
    sx_copy.start()

    link_copies = []
    for d in range(1, 8):
        dest = (t + d) & 7
        for i, ref in enumerate((fat_ref, naik_ref)):
            c = remote(ref.at[:, pl.ds(0, 6), dest], lraw.at[t, i],
                       l_send.at[i, d - 1], l_recv.at[i, d - 1], (dest, s))
            link_copies.append(c)

    def local_pass(n, h):
        def step(i, _):
            x = i >> 1
            base = 24 * h + (i & 1) * 12
            field = [[yy[n, 1 + x, base + v * 3 + c] for c in range(3)] for v in range(4)]
            acc = [[jnp.zeros((8, 128), F32)] * 3 for _ in range(4)]
            for d in range(4):
                links = [syz[x, d, e] for e in range(9)]
                for v in range(4):
                    if d == 0:
                        moved = [ahead_y(f) for f in field[v]]
                    elif d == 1:
                        moved = [behind_y(f) for f in field[v]]
                    else:
                        moved = [lanes(f, zp_i if d == 2 else zm_i) for f in field[v]]
                    acc[v] = mul_add(acc[v], links, moved, d & 1)
            for v in range(4):
                for c in range(3):
                    hh[x, base + v * 3 + c] = acc[v][c]
            return 0

        lax.fori_loop(0, 8, step, 0)

    def x_pass(n, h, plane_of, count, finish):
        def step(i, _):
            x = plane_of(i >> 1)
            base = 24 * h + (i & 1) * 12
            for back in (False, True):
                links = [sx[x if back else 1 + x, e] for e in range(9)]
                for v in range(4):
                    field = [yy[n, x if back else 2 + x, base + v * 3 + c] for c in range(3)]
                    acc = [hh[x, base + v * 3 + c] for c in range(3)] if not back else keep[v]
                    acc = mul_add(acc, links, field, back)
                    if not back:
                        if v == 0:
                            keep = []
                        keep.append(acc)
                    else:
                        for c in range(3):
                            finish(x, base + v * 3 + c, acc[c])
            return 0

        lax.fori_loop(0, 2 * count, step, 0)

    lflat = lraw.reshape(8 * 192, 128)

    def place_links(i, _):
        kind = i >> 2
        mu = i & 3
        for x in range(4):
            tiles = []
            for e in range(6):
                v = lanes(lflat[pl.ds(i * 24 + e * 4 + x, 8, stride=192), :], ix[SKL])
                tiles.append(rows(v, ix[SUB]))
            for a in range(3):
                b, c = (a + 1) % 3, (a + 2) % 3
                tiles.append(tiles[b] * tiles[3 + c] - tiles[c] * tiles[3 + b])
            for e in range(9):
                tl[x, kind, mu, e] = tiles[e]
        return 0

    for n in range(3):
        for h in range(2):
            local_pass(n, h)
            if n == 0 and h == 0:
                sx_copy.wait()
            if n == 2 and h == 0:
                for c in own_links + link_copies:
                    c.wait()
                lax.fori_loop(0, 8, place_links, 0)
                link_halos = [
                    remote(tl.at[3, 0, 0], tx.at[0, 3], lh_send.at[0, 0], lh_recv.at[0, 0], nxt),
                    remote(tl.at[pl.ds(1, 3), 1, 0], tx.at[1, pl.ds(1, 3)], lh_send.at[0, 1], lh_recv.at[0, 1], nxt),
                    remote(tl.at[:, 0, 1, :, pl.ds(7, 1)], tyh.at[0, :, :, pl.ds(7, 1)],
                           lh_send.at[1, 0], lh_recv.at[1, 0], ynxt),
                    remote(tl.at[:, 1, 1, :, pl.ds(5, 3)], tyh.at[1, :, :, pl.ds(5, 3)],
                           lh_send.at[1, 1], lh_recv.at[1, 1], ynxt),
                ]
            end(halos[h])

            def finish(x, comp, acc, n=n):
                if n == 0:
                    value = (-0.5 / HALF_WIDTH) * yy[0, 1 + x, comp] - (1.0 / HALF_WIDTH) * acc
                else:
                    value = ((-1.0 / HALF_WIDTH) * yy[n, 1 + x, comp] - (2.0 / HALF_WIDTH) * acc
                             - yy[n - 1, 1 + x, comp])
                yy[n + 1, 1 + x, comp] = value

            x_pass(n, h, lambda i: 3 * i, 2, finish)
            if n < 2:
                halos[h] = begin(halo(n + 1, h))
            if n == 0 and h == 0:
                begin(link_copies)
            if n == 2 and h == 0:
                begin(link_halos)
            x_pass(n, h, lambda i: 1 + i, 2, finish)

    def products(left, right):
        def step(k, _):
            mine = [left(x, k * 3 + c) for x in range(4) for c in range(3)]
            for d in range(9):
                j = (k + d) & 15
                total = None
                for x in range(4):
                    for c in range(3):
                        term = mine[x * 3 + c] * right(x, j * 3 + c)
                        total = term if total is None else total + term
                total = jnp.sum(total, axis=0, keepdims=True)
                prod[pl.ds(j * 16 + k, 1), :] = total
                prod[pl.ds(k * 16 + j, 1), :] = total
            return 0

        lax.fori_loop(0, 16, step, 0)
        sums = lax.dot_general(jnp.ones((8, 128), F32), prod[...], (((1,), (1,)), ((), ())),
                               precision=HIGH, preferred_element_type=F32)
        return jnp.where(row == 0, sums[:, :128], sums[:, 128:])

    def to_partner(buf, which):
        return remote(buf.at[0], buf.at[1], c_send.at[which], c_recv.at[which], partner)

    def to_chips(buf, which):
        return [remote(buf.at[chip], buf.at[chip], r_send.at[which, j], r_recv.at[which, j], chips[j])
                for j in range(7)]

    def to_times(buf, which):
        return [remote(buf.at[t], buf.at[t], t_send.at[which, j], t_recv.at[which, j], times[j])
                for j in range(7)]

    def total_of(buf):
        total = buf[0]
        for j in range(1, 8):
            total = total + buf[j]
        return total

    gone[0] = products(lambda x, e: yy[3, 1 + x, e], lambda x, e: yy[3, 1 + x, e])
    g_partner = to_partner(gone, 0)
    g_partner.start()
    def pack(i, _):
        x = i >> 3
        pair = i & 7
        idx = ix[PK + (x & 1)]
        for c in range(3):
            one = lanes(yy[3, 1 + x, pair * 3 + c], idx)
            two = lanes(yy[3, 1 + x, pair * 3 + 24 + c], idx)
            fs[pl.ds(x * 24 + pair * 3 + c, 8, stride=96), :] = jnp.where(high_half, two, one)
        return 0

    lax.fori_loop(0, 32, pack, 0)

    def part(ref, which):
        return ref.at[pl.ds(pl.multiple_of(which * 96, 96), 96)]

    f_copies = [
        remote(part(fs, (t + d) & 7), part(fr, t), f_send.at[d - 1], f_recv.at[d - 1], times[d - 1])
        for d in range(1, 8)
    ]
    f_local = pltpu.make_async_copy(part(fs, t), part(fr, t), f_own)

    g_partner.wait()
    gslot[chip] = gone[0] + gone[1]
    g_chips = to_chips(gslot, 0)
    for c in g_chips:
        c.start()
    for c in f_copies + [f_local]:
        c.start()

    halos = [begin(halo(3, h)) for h in range(2)]
    chunk = lane >> 4

    def fill_links(i, _):
        x = i & 3
        e = i >> 2
        xsign = (1 - 2 * (x & 1)).astype(F32)
        ysign = (1 - 2 * (row & 1)).astype(F32)
        tsign = (1 - 2 * (chunk & 1)).astype(F32)
        for kind, hop, weight in ((0, 1, 0.5 * ONE_HOP), (1, 3, 0.5 * THREE_HOP)):
            px = x - hop
            own = [tl[x, kind, mu, e] for mu in range(4)]
            before_x = jnp.where(px >= 0, tl[jnp.maximum(px, 0), kind, 0, e],
                                 tx[kind, jnp.minimum(px + 4, 3), e])
            before_y = pltpu.roll(jnp.where(row < 8 - hop, own[1], tyh[kind, x, e]), hop, 0)
            for pi in range(2):
                rho = (x + pi) & 1
                cc = ix[CC + rho]
                ct = ix[(CT3 if kind else CT1) + rho]
                cz = ix[(CZ3 if kind else CZ1) + rho]
                pis = -1.0 if pi else 1.0
                scale = [
                    jnp.full((8, 128), weight, F32),
                    jnp.full((8, 128), weight, F32) * xsign,
                    weight * xsign * ysign,
                ]
                fwd = [lanes(own[mu], cc) for mu in range(4)]
                bwd = [lanes(before_x, cc), lanes(before_y, ct), lanes(own[2], cz), lanes(own[3], ct)]
                for mu in range(4):
                    if mu < 3:
                        up, down = scale[mu], -scale[mu]
                    else:
                        up = jnp.where(chunk < 8 - hop, (pis * weight) * tsign, 0.0)
                        down = jnp.where(chunk >= hop, (-pis * weight) * tsign, 0.0)
                    ll[pi, x, (mu * 2 + kind) * 2, e] = up * fwd[mu]
                    ll[pi, x, (mu * 2 + kind) * 2 + 1, e] = down * bwd[mu]
        return 0

    end(link_halos)
    lax.fori_loop(0, 12, fill_links, 0)

    for c in g_chips:
        c.wait()
    gtm[t] = total_of(gslot)
    g_times = to_times(gtm, 0)
    for c in g_times:
        c.start()
    lax.fori_loop(12, 36, fill_links, 0)

    for c in f_copies:
        c.wait()
    f_local.wait()

    def unpack(i, _):
        x = i >> 1
        for c in range(12):
            e = (i & 1) * 12 + c
            v = rows(fr[pl.ds(x * 24 + e, 8, stride=96), :], ix[SUB])
            fp[x, e] = lanes(v, ix[DSK])
            fps[x, e] = lanes(v, ix[DSKS])
        return 0

    lax.fori_loop(0, 8, unpack, 0)

    for c in g_times:
        c.wait()

    flat = gtm.reshape(64, 128)
    for half in range(2):
        cb[pl.ds(128 * half, 128), :] = lax.dot_general(
            flat[pl.ds(half, 8, stride=8), :], jnp.where(chunk == row, 1.0, 0.0).astype(F32),
            (((0,), (0,)), ((), ())), precision=HIGH, preferred_element_type=F32)
    cols = [cb[pl.ds(16 * m, 16), :] * (1.0 / SITES) for m in range(16)]
    line = lax.broadcasted_iota(jnp.int32, (16, 128), 0)
    inv = [jnp.where(line == m, 1.0, 0.0).astype(F32) for m in range(16)]
    for j in range(16):
        scale = 1.0 / jnp.sqrt(cols[j][j:j + 1])
        factor = jnp.where(line > j, cols[j] * scale, 0.0)
        for m in range(j + 1, 16):
            cols[m] = cols[m] - factor * (cols[m][j:j + 1] * scale)
        for m in range(j + 1):
            top = inv[m][j:j + 1] * scale
            inv[m] = jnp.where(line == j, top, inv[m] - factor * top)
    for m in range(16):
        cb[pl.ds(16 * m, 16), :] = inv[m]

    def entry(k, j):
        return jnp.broadcast_to(cb[pl.ds(16 * j + k, 1), :], (8, 128))

    def d_halo(n, h):
        part = pl.ds(12 * h, 12)
        return [
            remote(ee.at[n, pl.ds(4, 3), part], ee.at[n, pl.ds(0, 3), part],
                   dx_send.at[n, h, 0], dx_recv.at[n, h, 0], nxt),
            remote(ee.at[n, pl.ds(3, 3), part], ee.at[n, pl.ds(7, 3), part],
                   dx_send.at[n, h, 1], dx_recv.at[n, h, 1], prv),
            remote(ee.at[n, pl.ds(3, 4), part, pl.ds(5, 3)], hp.at[n, :, part, pl.ds(5, 3)],
                   dy_send.at[n, h, 0], dy_recv.at[n, h, 0], ynxt),
            remote(ee.at[n, pl.ds(3, 4), part, pl.ds(0, 3)], hn.at[n, :, part, pl.ds(0, 3)],
                   dy_send.at[n, h, 1], dy_recv.at[n, h, 1], yprv),
        ]

    d_copies = [None, None]
    for pair in range(8):
        same = [jnp.where(high_half, entry(pair + 8, j + 8), entry(pair, j)) for j in range(pair + 1)]
        cross = [jnp.where(high_half, entry(pair + 8, j), 0.0) for j in range(8)]

        def mix(x, total, pair=pair, same=same, cross=cross):
            for c in range(3):
                value = cross[0] * fps[x, c]
                for j in range(1, 8):
                    value = value + cross[j] * fps[x, j * 3 + c]
                for j in range(pair + 1):
                    value = value + same[j] * fp[x, j * 3 + c]
                ee[0, 3 + x, pair * 3 + c] = value
                total = total + value * value
            return total

        mom[0, pair] = lax.fori_loop(0, 4, mix, jnp.zeros((8, 128), F32))
        if pair & 3 == 3:
            d_copies[pair >> 2] = begin(d_halo(0, pair >> 2))

    def inner_pass(n, h, pi):
        def step(i, _):
            x = i
            base = 12 * h
            rho = (x + pi) & 1
            field = [[ee[n, 3 + x, base + v * 3 + c] for c in range(3)] for v in range(4)]
            acc = [[jnp.zeros((8, 128), F32)] * 3 for _ in range(4)]
            for d in range(8, 16):
                links = [ll[pi, x, d, e] for e in range(9)]
                hop = 3 if (d >> 1) & 1 else 1
                if d < 12:
                    idx = ix[ZZ + rho * 4 + (d - 8)]
                for v in range(4):
                    if d < 12:
                        moved = [lanes(f, idx) for f in field[v]]
                    else:
                        shift = 16 * hop if d & 1 else 128 - 16 * hop
                        moved = [pltpu.roll(f, shift, 1) for f in field[v]]
                    acc[v] = mul_add(acc[v], links, moved, d & 1)
            for v in range(4):
                for c in range(3):
                    h2[x, base + v * 3 + c] = acc[v][c]
            return 0

        lax.fori_loop(0, 4, step, 0)

    def outer_pass(n, h, pi, store):
        for v in range(4):
            mom[n + 1, 4 * h + v] = jnp.zeros((8, 128), F32)

        def step(i, _):
            x = i
            base = 12 * h
            acc = [[h2[x, base + v * 3 + c] for c in range(3)] for v in range(4)]
            for d in range(8):
                links = [ll[pi, x, d, e] for e in range(9)]
                hop = 3 if (d >> 1) & 1 else 1
                for v in range(4):
                    comps = [base + v * 3 + c for c in range(3)]
                    if d < 4:
                        moved = [ee[n, 3 + x - hop if d & 1 else 3 + x + hop, e] for e in comps]
                    elif d & 1:
                        moved = [pltpu.roll(jnp.where(row < 8 - hop, ee[n, 3 + x, e], hp[n, x, e]), hop, 0)
                                 for e in comps]
                    else:
                        moved = [pltpu.roll(jnp.where(row >= hop, ee[n, 3 + x, e], hn[n, x, e]), 8 - hop, 0)
                                 for e in comps]
                    acc[v] = mul_add(acc[v], links, moved, d & 1)
            for v in range(4):
                for c in range(3):
                    if store:
                        ee[n + 1, 3 + x, base + v * 3 + c] = acc[v][c]
                mom[n + 1, 4 * h + v] += (
                    acc[v][0] * acc[v][0] + acc[v][1] * acc[v][1] + acc[v][2] * acc[v][2])
            return 0

        lax.fori_loop(0, 4, step, 0)

    def flat_to_square(tile):
        total = jnp.zeros((16, 128), F32)
        for m in range(16):
            piece = jnp.broadcast_to(tile[m >> 3:(m >> 3) + 1], (16, 128))
            piece = pltpu.roll(piece, (128 - 16 * (m & 7)) & 127, 1) if m & 7 else piece
            total = jnp.where(line == m, piece, total)
        return total[:, :16]

    for n in range(3):
        pi = 1 - (n & 1)
        inner_pass(n, 0, pi)
        if n == 1:
            def keep_image(x, comp, acc):
                af[x, comp] = 6.0 * yy[3, 1 + x, comp] - acc

            for g in range(2):
                local_pass(3, g)
                end(halos[g])
                x_pass(3, g, lambda i: i, 4, keep_image)
        if n == 1:
            sone[0, 1] = products(lambda x, e: yy[3, 1 + x, e], lambda x, e: af[x, e])
        for h in range(2):
            if h == 1:
                inner_pass(n, 1, pi)
            end(d_copies[h])
            outer_pass(n, h, pi, n < 2)
            if n < 2:
                d_copies[h] = begin(d_halo(n + 1, h))

    saved = [pltpu.make_async_copy(ee.at[2 * i, pl.ds(3, 4)], ref, out_sem.at[i])
             for i, ref in enumerate((source_ref, second_ref))]
    for c in saved:
        c.start()

    prod[...] = jnp.zeros((256, 128), F32)
    for m in range(4):
        for pair in range(8):
            prod[pl.ds(8 * m + pair, 1), :] = jnp.sum(mom[m, pair], axis=0, keepdims=True)
    select = jnp.where(((lane >> 3) & 1) == row, 1.0, 0.0).astype(F32)
    sone[0, 0] = lax.dot_general(select, prod[pl.ds(0, 128), :], (((1,), (1,)), ((), ())),
                              precision=HIGH, preferred_element_type=F32)
    s_partner = to_partner(sone, 1)
    s_partner.start()
    s_partner.wait()
    sslot[chip] = sone[0] + sone[1]
    s_chips = to_chips(sslot, 1)
    for c in s_chips:
        c.start()
    for c in s_chips:
        c.wait()
    both = total_of(sslot)
    stm[t] = both[0]
    s_times = to_times(stm, 1)
    for c in s_times:
        c.start()

    square = flat_to_square(both[1])
    pick = jnp.where(lane == t * 16, 1.0, 0.0).astype(F32)
    weights = lax.dot_general(pick, cb[...], (((1,), (1,)), ((), ())),
                              precision=HIGH, preferred_element_type=F32)
    weights = flat_to_square(jnp.where(row == 0, weights[:, :128], weights[:, 128:]))
    half = lax.dot_general(weights, square, (((0,), (0,)), ((), ())),
                           precision=HIGH, preferred_element_type=F32)
    proj_ref[0] = lax.dot_general(half, weights, (((1,), (0,)), ((), ())),
                                  precision=HIGH, preferred_element_type=F32) * (1.0 / SITES)
    for c in s_times:
        c.wait()
    n0 = total_of(stm)
    n1 = pltpu.roll(n0, 120, 1)
    n2 = pltpu.roll(n0, 112, 1)
    n3 = pltpu.roll(n0, 104, 1)
    ratio = n1 / n0
    alpha0 = 1.0 / (0.25 + ratio)
    rr = alpha0 * alpha0 * (n2 - ratio * n1)
    beta = rr / n0
    a = alpha0 * ratio + beta
    energy = 0.25 * rr * (1.0 + beta) + a * a * n1 - 2.0 * a * alpha0 * n2 + alpha0 * alpha0 * n3
    alpha1 = rr / energy
    weight_ref[...] = jnp.where(row < 2, alpha1 * alpha0, pltpu.roll(alpha0 + alpha1 * a, 2, 0))
    for c in saved:
        c.wait()


def assemble(proj_ref, source_ref, second_ref, weight_ref, done_ref, out_ref,
             small, weights, pp, ww, full, in_sem, out_sem):
    loads = [pltpu.make_async_copy(weight_ref, weights, in_sem.at[0]),
             pltpu.make_async_copy(proj_ref, small, in_sem.at[1])]
    parts = [pl.ds(12 * i, 12) for i in range(2)]
    fields = [
        [pltpu.make_async_copy(ref.at[:, part], buf.at[:, part], in_sem.at[2 + 2 * i + j])
         for j, (ref, buf) in enumerate(((source_ref, pp), (second_ref, ww)))]
        for i, part in enumerate(parts)
    ]
    for c in loads + sum(fields, []):
        c.start()
    row, lane = tile_iota()
    high_half = (lane & 8) != 0
    spots = [(lane & 112) | 8 * h | ((lane & 15) >> 1) for h in range(2)]
    even = [((x + row + (lane >> 4) + lane) & 1) == 0 for x in range(2)]
    for c in loads:
        c.wait()
    done = pltpu.make_async_copy(small, done_ref, out_sem.at[0])
    done.start()
    stores = [done]

    def spread(first, pair):
        low = jnp.broadcast_to(weights[first:first + 1, pair:pair + 1], (8, 128))
        high = jnp.broadcast_to(weights[first + 1:first + 2, pair:pair + 1], (8, 128))
        return jnp.where(high_half, high, low)

    for i in range(2):
        for c in fields[i]:
            c.wait()
        for pair in range(4 * i, 4 * i + 4):
            ca = spread(2, pair)
            cd = spread(0, pair)
            for x in range(4):
                for c in range(3):
                    value = ca * pp[x, pair * 3 + c] + cd * ww[x, pair * 3 + c]
                    for h in range(2):
                        full[pair + 8 * h, c, x] = jnp.where(even[x & 1], lanes(value, spots[h]), 0.0)
        for h in range(2):
            where = pl.ds(8 * h + 4 * i, 4)
            copy = pltpu.make_async_copy(full.at[where], out_ref.at[where], out_sem.at[1 + 2 * i + h])
            copy.start()
            stores.append(copy)
    for c in stores:
        c.wait()


def rows_first(array, lead):
    return array.reshape(lead, 4, 8, 128).transpose(0, 2, 1, 3)


def body(start, smear_links, fat_links, naik_links):
    start = rows_first(start, 48).reshape(1536, 128)
    smear = rows_first(smear_links, 27).reshape(864, 128)
    fat = rows_first(fat_links, 36).reshape(4, 9, 8, 4, 128)
    naik = rows_first(naik_links, 36).reshape(4, 9, 8, 4, 128)
    vm = lambda *shape: pltpu.VMEM(shape, F32)
    dma = lambda *shape: pltpu.SemaphoreType.DMA(shape) if shape else pltpu.SemaphoreType.DMA
    anywhere = pl.BlockSpec(memory_space=pl.ANY)
    local = pl.BlockSpec(memory_space=pltpu.VMEM)
    packed = jax.ShapeDtypeStruct((4, 24, 8, 128), F32)
    parts = pl.pallas_call(
        kernel,
        out_shape=(jax.ShapeDtypeStruct((1, 16, 16), F32), packed, packed,
                   jax.ShapeDtypeStruct((8, 128), F32)),
        in_specs=[anywhere] * 4,
        out_specs=(local, anywhere, anywhere, local),
        scratch_shapes=[
            vm(1536, 128), vm(864, 128), vm(4, 6, 48, 8, 128), vm(5, 9, 8, 128), vm(4, 4, 9, 8, 128),
            vm(4, 48, 8, 128), vm(4, 48, 8, 128), vm(256, 128), vm(768, 128), vm(768, 128),
            vm(8, 2, 4, 6, 4, 128),
            vm(4, 2, 4, 9, 8, 128), vm(2, 4, 9, 8, 128), vm(2, 4, 9, 8, 128), vm(2, 4, 16, 9, 8, 128),
            vm(3, 10, 24, 8, 128), vm(3, 4, 24, 8, 128), vm(3, 4, 24, 8, 128), vm(4, 24, 8, 128),
            vm(4, 24, 8, 128), vm(4, 24, 8, 128), pltpu.VMEM((SLOTS, 8, 128), jnp.int32),
            vm(256, 128), vm(4, 8, 8, 128),
            vm(2, 8, 128), vm(8, 8, 128), vm(8, 8, 128),
            vm(2, 2, 8, 128), vm(8, 2, 8, 128), vm(8, 8, 128),
            dma(2), dma(4, 2, 2), dma(4, 2, 2), dma(), dma(), dma(2, 7), dma(2, 7), dma(2),
            dma(2, 2), dma(2, 2), dma(7), dma(7), dma(),
            dma(3, 2, 2), dma(3, 2, 2), dma(3, 2, 2), dma(3, 2, 2),
            dma(2), dma(2), dma(2, 7), dma(2, 7), dma(2, 7), dma(2, 7), dma(2),
        ],
        compiler_params=pltpu.CompilerParams(
            collective_id=0, has_side_effects=True, vmem_limit_bytes=60 * 2**20),
        name="distill",
    )(start, smear, fat, naik)
    return pl.pallas_call(
        assemble,
        out_shape=(jax.ShapeDtypeStruct((1, 16, 16), F32),
                   jax.ShapeDtypeStruct((16, 3, 4, 8, 128), F32)),
        in_specs=[anywhere] * 4,
        out_specs=(anywhere, anywhere),
        scratch_shapes=[vm(1, 16, 16), vm(8, 128), vm(4, 24, 8, 128), vm(4, 24, 8, 128),
                        vm(16, 3, 4, 8, 128), dma(10), dma(9)],
        compiler_params=pltpu.CompilerParams(vmem_limit_bytes=60 * 2**20),
        name="assemble",
    )(*parts)


def solution(mesh):
    in_specs = (
        P(None, None, "tm", "space", None),
        P(None, None, None, "tm", "space", None),
        P(None, None, None, "tm", "space", None),
        P(None, None, None, "tm", "space", None),
    )
    out_specs = (P("tm", None, None), P(None, None, "space", "tm", None))
    return jax.shard_map(body, mesh=mesh, in_specs=in_specs, out_specs=out_specs, check_vma=False)
```
